256 devices in a mesh: lon: 32 (over y_lo, z, core), lat: 8 (over y_hi, x).
Axes of the slice: x: 4, y: 4 (y_hi: 2, y_lo: 2; y = y_hi * 2 + y_lo), z: 8, core: 2. Of those that a mesh axis runs over, the one named last changes fastest.
Arguments:
- tracer: float32 [192, 2880, 128], P('lat', 'lon'), may hold values from -6 to 6
- wind_u: float32 [192, 2880, 128], P('lat', 'lon'), may hold values from -0.9 to 0.9
- wind_v: float32 [192, 2880, 128], P('lat', 'lon'), may hold values from -0.9 to 0.9
- cotangent: float32 [192, 2880, 128], P('lat', 'lon'), may hold values from -6 to 6
- cutoff: int32 [192], P('lat'), may hold values from 1 to 1440, as said below
Outputs:
- advanced: float32 [192, 2880, 128], P('lat', 'lon')
- grad_tracer: float32 [192, 2880, 128], P('lat', 'lon')
- grad_u: float32 [192, 2880, 128], P('lat', 'lon')
- grad_v: float32 [192, 2880, 128], P('lat', 'lon')
The draws below stay inside these ranges and needn't reach their ends.
Inputs may be any that keep to these rules, and one draw needn't show every extreme that they name: cutoff is 1440 on every latitude except the 12 nearest each pole, where it rises from 1 on the latitude next to the pole and stays below 1440.
All inputs are finite; a program needn't handle non-finite values.
Results may differ from the reference program's by a relative error of at most 0.00007.
Values sent between devices are 32-bit elements; how exact they have to be, the bound alone decides.
No kernel may reach another device: no remote copies, remote signals or barrier semaphores. Data moves between devices by JAX's collectives and lax.ppermute only.
A program may use at most 128 MiB of HBM per device.

```python
import jax
import jax.numpy as jnp

NLON = 2880
LEV = 128
NLAT = 192
POLAR = 12


def draw_cutoff(key, part):
    key = jax.random.fold_in(key, 11)
    latitudes = jnp.arange(NLAT, dtype=jnp.int32)
    nearest = jnp.minimum(latitudes, NLAT - 1 - latitudes)
    base_value = 1 + (NLON // 2 - 2) * nearest // POLAR
    jitter = jax.random.randint(key, (NLAT,), 0, NLON // (4 * POLAR) + 1, dtype=jnp.int32)
    jitter = jnp.where(nearest > 0, jitter, 0)
    limited = jnp.minimum(base_value + jitter, NLON // 2 - 1)
    return jnp.where(nearest < POLAR, limited, NLON // 2).astype(jnp.int32)


def shard_levels(rng, extent, shards, low, largest):
    factor_of, own = 1.0, jax.random.fold_in(rng, 6)
    for dim, parts in shards:
        steps = jnp.exp(jax.random.uniform(jax.random.fold_in(own, dim), (parts,), jnp.float32, low / len(shards), largest / len(shards)))
        factor_of = factor_of * jnp.repeat(steps, extent[dim] // parts).reshape([-1 if axis == dim else 1 for axis in range(len(extent))])
    return factor_of


def centred(own_key, shape, spread, reach, pieces=(), kind=jnp.bfloat16):
    values = spread * jax.random.normal(own_key, shape, jnp.float32)
    if pieces:
        values = values * shard_levels(own_key, shape, pieces, -0.22, 0.18)
    return jnp.clip(values, -reach, reach).astype(kind)


def setup_inputs(seed: int = 0) -> dict:
    splits = jax.random.split(jax.random.key(seed), 6)
    tracer = centred(splits[0], (NLAT, NLON, LEV), 1.0, 6.0, ((0, 8), (1, 32)), jnp.float32)
    wind_u = jnp.clip(jax.random.uniform(splits[1], (NLAT, NLON, LEV), jnp.float32, -0.9, 0.9) * shard_levels(splits[1], (NLAT, NLON, LEV), ((0, 8), (1, 32)), -0.4, 0.0), -0.9, 0.9)
    wind_v = jnp.clip(jax.random.uniform(splits[2], (NLAT, NLON, LEV), jnp.float32, -0.9, 0.9) * shard_levels(splits[2], (NLAT, NLON, LEV), ((0, 8), (1, 32)), -0.4, 0.0), -0.9, 0.9)
    cotangent = centred(splits[3], (NLAT, NLON, LEV), 1.0, 6.0, ((0, 8), (1, 32)), jnp.float32)
    cutoff = draw_cutoff(jax.random.fold_in(splits[5], 71), 0)
    return {"tracer": tracer, "wind_u": wind_u, "wind_v": wind_v, "cotangent": cotangent, "cutoff": cutoff}


DIFFUSION = 0.125


def neighbours(field, sign_value):
    east_side = jnp.roll(field, -1, axis=1)
    west_side = jnp.roll(field, 1, axis=1)
    opposite = jnp.roll(field, NLON // 2, axis=1)
    north_side = jnp.concatenate([sign_value * opposite[:1], field[:-1]], axis=0)
    south_side = jnp.concatenate([field[1:], sign_value * opposite[-1:]], axis=0)
    return east_side, west_side, north_side, south_side


def highpass(field, cutoff):
    spectrum = jnp.fft.rfft(field, axis=1)
    wavenumber = jnp.arange(NLON // 2 + 1, dtype=jnp.int32)
    kept_modes = (wavenumber[None, :] > cutoff[:, None])[:, :, None]
    return jnp.fft.irfft(jnp.where(kept_modes, spectrum, 0.0), n=NLON, axis=1).astype(field.dtype)


def reference(tracer, wind_u, wind_v, cotangent, cutoff):
    east_q, west_q, north_q, south_q = neighbours(tracer, 1.0)
    stepped = (tracer - 0.5 * wind_u * (east_q - west_q) - 0.5 * wind_v * (north_q - south_q)
               + DIFFUSION * (east_q + west_q + north_q + south_q - 4.0 * tracer))
    advanced = stepped - highpass(stepped, cutoff)
    adjoint = cotangent - highpass(cotangent, cutoff)
    flux_u = wind_u * adjoint
    flux_v = wind_v * adjoint
    east_a, west_a, north_a, south_a = neighbours(adjoint, 1.0)
    east_u, west_u, north_u, south_u = neighbours(flux_u, 1.0)
    east_v, west_v, north_v, south_v = neighbours(flux_v, -1.0)
    grad_tracer = (adjoint + 0.5 * (east_u - west_u) + 0.5 * (north_v - south_v)
                   + DIFFUSION * (east_a + west_a + north_a + south_a - 4.0 * adjoint))
    grad_u = -0.5 * (east_q - west_q) * adjoint
    grad_v = -0.5 * (north_q - south_q) * adjoint
    return advanced, grad_tracer, grad_u, grad_v
```

```python
import functools

import jax
import jax.numpy as jnp
import ml_dtypes
import numpy as np
from jax import lax
from jax.experimental import pallas as pl
from jax.experimental.pallas import tpu as pltpu
from jax.sharding import PartitionSpec as P

F32 = jnp.float32
BF16 = jnp.bfloat16
LON, LAT = 32, 8
ROWS, COLS, LEV = 24, 90, 128
NLON = LON * COLS
POLAR = 12
MODES = LON // 2 + 1
PAD = 96
SUB = PAD // 4
GROUPS = 5
VMEM = 32 * 1024 * 1024
WINDOW = 16
CHUNK = 15

SPREAD_A = ((0, 1), (7, 6))
SPREAD_B = ((0, 3), (7, 4))


def dft_tables():
    place = np.arange(PAD)
    inside = place < COLS
    wave = np.arange(PAD)
    angle = 2 * np.pi * (wave[:, None] * place[None, :] % COLS) / COLS
    live = (wave[:, None] < COLS) & inside[None, :]
    cos, sin = np.where(live, np.cos(angle), 0), np.where(live, np.sin(angle), 0)
    forward = np.block([[cos, sin], [-sin, cos]])

    where = np.where(inside, place, 0)
    where[91] = -1
    where[90] = COLS
    valid = place < COLS + 2
    back_angle = 2 * np.pi * (where[:, None] * wave[None, :] % COLS) / COLS
    back_live = valid[:, None] & (wave[None, :] < COLS)
    bcos, bsin = np.where(back_live, np.cos(back_angle), 0), np.where(back_live, np.sin(back_angle), 0)
    bcos[92, 0] = 1.0
    backward = np.block([[bcos, -bsin], [bsin, bcos]]) / NLON

    def packed(values):
        spread = values.reshape(MODES, 4, SUB).transpose(0, 2, 1)
        return np.repeat(spread, 32, axis=2).astype(np.float32)

    mode = np.arange(MODES)
    turn = 2 * np.pi * (mode[:, None] * np.where(inside, place, 0)[None, :] % NLON) / NLON
    back_turn = 2 * np.pi * (mode[:, None] * where[None, :] % NLON) / NLON
    back_on = np.where(valid[None, :], 1.0, 0.0) * np.ones((MODES, 1))
    back_on[0, 92] = 1.0
    twiddle = np.stack([packed(np.cos(turn)), packed(-np.sin(turn))])
    back_twiddle = np.stack([packed(np.cos(back_turn) * back_on), packed(np.sin(back_turn) * back_on)])

    def split(matrix):
        high = matrix.astype(ml_dtypes.bfloat16)
        low = (matrix - high.astype(np.float64)).astype(ml_dtypes.bfloat16)
        return np.stack([high, low]).astype(np.float32)

    return split(forward), split(backward), twiddle, back_twiddle


def swap_blocks(parts):
    lane = lax.broadcasted_iota(jnp.int32, parts[0].shape, 1)
    low_half, even_block = lane < 64, (lane // 32) % 2 == 0
    first = [None] * 4
    for i in (0, 1):
        a, b = parts[i], parts[i + 2]
        first[i] = jnp.where(low_half, a, pltpu.roll(b, 64, 1))
        first[i + 2] = jnp.where(low_half, pltpu.roll(a, 64, 1), b)
    second = [None] * 4
    for i in (0, 2):
        a, b = first[i], first[i + 1]
        second[i] = jnp.where(even_block, a, pltpu.roll(b, 32, 1))
        second[i + 1] = jnp.where(even_block, pltpu.roll(a, 96, 1), b)
    return second


def start_of(lat):
    return jnp.where(lat[0] == 0, 0, ROWS - POLAR)


def window_of(lat):
    return pl.multiple_of(jnp.where(lat[0] == 0, 0, ROWS - WINDOW), 8)


def line_of(ref, row, count=COLS, first=0):
    rows = ref.shape[1]
    return ref.reshape(ref.shape[0] * rows, LEV)[pl.ds(first * rows + row, count, stride=rows), :]


def shifted(x, above, below):
    rows = x.shape[0]
    place = lax.broadcasted_iota(jnp.int32, x.shape, 0)
    north = jnp.where(place == 0, above, pltpu.roll(x, 1, 0))
    south = jnp.where(place == rows - 1, below, pltpu.roll(x, rows - 1, 0))
    return north, south


def pack_rows(lat, cutoff, slabs, outs):
    first = start_of(lat) - window_of(lat)
    place = lax.broadcasted_iota(jnp.int32, (WINDOW, LEV), 0)
    cuts = jnp.zeros((WINDOW, LEV), F32)
    for k in range(POLAR):
        cuts = jnp.where(place == first + k, cutoff[start_of(lat) + k].astype(F32), cuts)
    for j in range(COLS, PAD - 1):
        slabs[j] = jnp.zeros((WINDOW, LEV), F32)
    slabs[PAD - 1] = cuts
    for k in range(POLAR):
        parts = [line_of(slabs, first + k, SUB, SUB * s) for s in range(4)]
        for q, part in enumerate(swap_blocks(parts)):
            outs[k // 4][4 * (k % 4) + q] = part


def borders(
    lat, t0, t1, c0, c1, u0, u1, tt0, tt1, ct0, ct1, vt0, vt1, first_cols, last_cols, first_rows, last_rows, edge
):
    for i, (first_col, last_col) in enumerate(((t0, t1), (c0, c1), (u0, u1))):
        first_cols[i] = first_col[0]
        last_cols[i] = last_col[0]
    for i, (first_tile, last_tile) in enumerate(((tt0, tt1), (ct0, ct1), (vt0, vt1))):
        first_rows[i] = line_of(first_tile, 0)
        last_rows[i] = line_of(last_tile, 7)
    is0 = lat[0] == 0
    for i, j in enumerate((0, 2)):
        edge[i] = jnp.where(is0, first_rows[j], last_rows[j])


def pack_cotangent(lat, cutoff, ct, out0, out1, out2, slabs):
    rows = pl.ds(window_of(lat), WINDOW)
    for j in range(COLS):
        slabs[j] = ct[j, rows, :]
    pack_rows(lat, cutoff, slabs, (out0, out1, out2))


def pack_stepped(lat, cutoff, tr, wu, wv, he, hw, ac, out0, out1, out2, slabs):
    rows = pl.ds(window_of(lat), WINDOW)

    def step(j, east, west):
        x = tr[j, rows, :]
        beyond = ac[0, pl.ds(j, 1), :]
        north, south = shifted(x, beyond, beyond)
        slabs[j] = (
            x
            - 0.5 * wu[j, rows, :] * (east - west)
            - 0.5 * wv[j, rows, :] * (north - south)
            + 0.125 * (east + west + north + south - 4.0 * x)
        )

    def middle(i, carry):
        for m in range(8):
            j = 8 * i + m + 1
            step(j, tr[j + 1, rows, :], tr[j - 1, rows, :])
        return carry

    step(0, tr[1, rows, :], hw[0, rows, :])
    lax.fori_loop(0, (COLS - 2) // 8, middle, 0)
    step(COLS - 1, he[0, rows, :], tr[COLS - 2, rows, :])
    pack_rows(lat, cutoff, slabs, (out0, out1, out2))


def times(a, cos, sin):
    if isinstance(sin, float) and sin == 0.0:
        return (a[0] * cos, None if a[1] is None else a[1] * cos) if cos != 1.0 else a
    if a[1] is None:
        return a[0] * cos, a[0] * sin
    return a[0] * cos - a[1] * sin, a[0] * sin + a[1] * cos


def plus(a, b):
    im = b[1] if a[1] is None else (a[1] if b[1] is None else a[1] + b[1])
    return a[0] + b[0], im


def minus(a, b):
    if a[1] is None:
        im = None if b[1] is None else -b[1]
    else:
        im = a[1] if b[1] is None else a[1] - b[1]
    return a[0] - b[0], im


def conj(a):
    return a[0], None if a[1] is None else -a[1]


def quarter(a, sign):
    re, im = a
    return (None if im is None else -sign * im), sign * re


def turned(a, k, n, sign):
    if k == 0:
        return a
    if 4 * k == n:
        re = jnp.zeros_like(a[0]) if a[1] is None else (-a[1] if sign > 0 else a[1])
        return re, (a[0] if sign > 0 else -a[0])
    return times(a, float(np.cos(2 * np.pi * k / n)), float(sign * np.sin(2 * np.pi * k / n)))


def real_dft(values):
    n = len(values)
    if n == 1:
        return [(values[0], None)]
    even, odd = real_dft(values[0::2]), real_dft(values[1::2])
    out = [None] * (n // 2 + 1)
    for k in range(n // 4 + 1):
        t = turned(odd[k], k, n, -1)
        out[k] = plus(even[k], t)
        if n // 2 - k != k:
            out[n // 2 - k] = conj(minus(even[k], t))
    return out


def real_inverse(modes):
    n = 2 * (len(modes) - 1)
    if n == 2:
        return [modes[0][0] + modes[1][0], modes[0][0] - modes[1][0]]
    even, odd = [], []
    for k in range(n // 4 + 1):
        a, b = modes[k], conj(modes[n // 2 - k])
        even.append(plus(a, b))
        odd.append(turned(minus(a, b), k, n, 1))
    out = [None] * n
    out[0::2], out[1::2] = real_inverse(even), real_inverse(odd)
    return out


def three_products(matrix, x):
    high = x.astype(BF16)
    low = (x - high.astype(F32)).astype(BF16)
    dot = functools.partial(jnp.dot, preferred_element_type=F32)
    main, rest = matrix[0].astype(BF16), matrix[1].astype(BF16)
    return dot(main, high) + (dot(main, low) + dot(rest, high))


def pick(lat, own_c, a_c, b_c, own_s, a_s, b_s, out, sems):
    polar = (lat[0] == 0) | (lat[0] == LAT - 1)
    in_a = (lat[0] == 1) | (lat[0] == LAT - 2)

    def copies(c, s):
        return [
            pltpu.make_async_copy(c, out.at[pl.ds(0, 16)], sems.at[0]),
            pltpu.make_async_copy(s, out.at[pl.ds(16, 16)], sems.at[1]),
        ]

    for chosen, c, s in (
        (polar, own_c, own_s),
        (in_a, a_c, a_s),
        (jnp.logical_not(polar | in_a), b_c, b_s),
    ):

        @pl.when(chosen)
        def _():
            for copy in copies(c, s):
                copy.start()

    for copy in copies(own_c, own_s):
        copy.wait()


def keep_low(x, forward, backward, twiddle, back_twiddle, out, lines, rhs):
    lane = lax.broadcasted_iota(jnp.int32, (8, LEV), 1)
    spot = lax.broadcasted_iota(jnp.int32, (8, LEV), 0)
    cut = jnp.max(jnp.where((lane >= 96) & (spot == 7), x[0, SUB - 8 : SUB, :], 0.0))
    for i in range(SUB // 8):
        at = slice(8 * i, 8 * i + 8)
        modes = real_dft([x[b, at, :] for b in range(LON)])
        for k, mode in enumerate(modes):
            re, im = times(mode, twiddle[0, k, at, :], twiddle[1, k, at, :])
            lines[0, k, at, :] = re
            lines[1, k, at, :] = im
    zero = jnp.zeros((SUB, LEV), F32)
    for g in range(GROUPS):
        for part in range(2):
            stack = [lines[part, 4 * g + m] if 4 * g + m < MODES else zero for m in range(4)]
            for s, block in enumerate(swap_blocks(stack)):
                rhs[PAD * part + SUB * s : PAD * part + SUB * s + SUB, LEV * g : LEV * g + LEV] = block
    spectrum = three_products(forward, rhs[...])
    shape = (PAD, LEV * GROUPS)
    number = 4 * (lax.broadcasted_iota(jnp.int32, shape, 1) // LEV)
    number = number + (lax.broadcasted_iota(jnp.int32, shape, 1) // 32) % 4
    number = number + 32 * lax.broadcasted_iota(jnp.int32, shape, 0)
    kept = jnp.minimum(number, NLON - number).astype(F32) <= cut
    kept = jnp.concatenate([kept.astype(F32)] * 2, axis=0) > 0.5
    rhs[...] = three_products(backward, jnp.where(kept, spectrum, 0.0))
    for g in range(GROUPS):
        for part in range(2):
            stack = [
                rhs[PAD * part + SUB * s : PAD * part + SUB * s + SUB, LEV * g : LEV * g + LEV]
                for s in range(4)
            ]
            for m, block in enumerate(swap_blocks(stack)):
                if 4 * g + m < MODES:
                    lines[part, 4 * g + m] = block
    for i in range(SUB // 8):
        at = slice(8 * i, 8 * i + 8)
        modes = [
            times(
                (lines[0, k, at, :], lines[1, k, at, :]),
                back_twiddle[0, k, at, :],
                back_twiddle[1, k, at, :],
            )
            for k in range(MODES)
        ]
        for b, value in enumerate(real_inverse(modes)):
            out[b, at, :] = value


def outputs(
    lat, ret0, ret1, ret2, tr, wu, wv, ct, he, hw, n3, s3, ac,
    adv, gt, gu, gv, adjoint, low_stepped, top, bottom,
):
    is0, is7 = lat[0] == 0, lat[0] == LAT - 1
    step = pl.program_id(0)
    rets = (ret0, ret1, ret2)
    start = start_of(lat)

    @pl.when(step == 0)
    def _():
        def fill(i, carry):
            for m in range(10):
                adjoint[10 * i + m] = ct[10 * i + m]
            return carry

        lax.fori_loop(0, COLS // 10, fill, 0)
        adjoint[COLS] = he[1]
        adjoint[COLS + 1] = hw[1]

        @pl.when(is0 | is7)
        def _():
            flat = adjoint.reshape(PAD * ROWS, LEV)
            flat_stepped = low_stepped.reshape(PAD * ROWS, LEV)
            for k in range(POLAR):
                ret, kk = rets[k // 4], k % 4
                for target, base in ((flat, 0), (flat_stepped, 16)):
                    line = swap_blocks([ret[base + 4 * kk + q] for q in range(4)])
                    for s, part in enumerate(line):
                        target[pl.ds(SUB * s * ROWS + start + k, SUB, stride=ROWS), :] = part

        outer = jnp.where(is0, 0, ROWS - 1)
        mean = adjoint[COLS + 2, pl.ds(outer, 1), :]
        opposite = 2.0 * mean - line_of(adjoint, outer)
        top[0] = jnp.where(is0, ac[0], n3[0])
        top[1] = jnp.where(is0, (0.125 - 0.5 * ac[1]) * opposite, (0.125 + 0.5 * n3[2]) * n3[1])
        bottom[0] = jnp.where(is7, ac[0], s3[0])
        bottom[1] = jnp.where(is7, (0.125 + 0.5 * ac[1]) * opposite, (0.125 - 0.5 * s3[2]) * s3[1])

    place = lax.broadcasted_iota(jnp.int32, (ROWS, LEV), 0)
    filtered = (is0 & (place < POLAR)) | (is7 & (place >= ROWS - POLAR))
    base = step * CHUNK

    for m in range(CHUNK):
        j = base + m
        one = pl.ds(j, 1)
        x, u, v, a = tr[j], wu[j], wv[j], adjoint[j]
        if m == 0:
            at_edge = step == 0
            before = jnp.maximum(j - 1, 0)
            west = jnp.where(at_edge, hw[0], tr[before])
            u_west = jnp.where(at_edge, hw[2], wu[before])
            a_west = adjoint[jnp.where(at_edge, COLS + 1, before)]
        else:
            west, u_west, a_west = tr[j - 1], wu[j - 1], adjoint[j - 1]
        a_east = adjoint[j + 1]
        if m == CHUNK - 1:
            at_edge = j == COLS - 1
            beyond = jnp.minimum(j + 1, COLS - 1)
            east = jnp.where(at_edge, he[0], tr[beyond])
            u_east = jnp.where(at_edge, he[2], wu[beyond])
        else:
            east, u_east = tr[j + 1], wu[j + 1]
        north, south = shifted(x, top[0, one, :], bottom[0, one, :])
        across, along = east - west, north - south
        stepped = (
            x - 0.5 * u * across - 0.5 * v * along + 0.125 * (east + west + north + south - 4.0 * x)
        )
        adv[m] = jnp.where(filtered, low_stepped[j], stepped)
        half = -0.5 * a
        gu[m] = across * half
        gv[m] = along * half
        place_north = jnp.where(
            place == 0, top[1, one, :], pltpu.roll((0.125 + 0.5 * v) * a, 1, 0)
        )
        place_south = jnp.where(
            place == ROWS - 1, bottom[1, one, :], pltpu.roll((0.125 - 0.5 * v) * a, ROWS - 1, 0)
        )
        gt[m] = (
            0.5 * a
            + (0.125 + 0.5 * u_east) * a_east
            + (0.125 - 0.5 * u_west) * a_west
            + place_north
            + place_south
        )


def whole(*shape):
    return pl.BlockSpec(shape, lambda i, *m: (0,) * len(shape))


def column(j):
    return pl.BlockSpec((1, ROWS, LEV), lambda i, *m: (j, 0, 0))


FULL = whole(COLS, ROWS, LEV)
FIRST_TILES = pl.BlockSpec((COLS, 8, LEV), lambda i, *m: (0, 0, 0))
LAST_TILES = pl.BlockSpec((COLS, 8, LEV), lambda i, *m: (0, ROWS // 8 - 1, 0))
OUTER_TILES = pl.BlockSpec(
    (COLS, 8, LEV), lambda i, lat, *m: (0, jnp.where(lat[0] == 0, 0, ROWS // 8 - 1), 0)
)
OUT = pl.BlockSpec((CHUNK, ROWS, LEV), lambda i, *m: (i, 0, 0))
LINES = whole(16, SUB, LEV)
UNITS = whole(32, SUB, LEV)
EDGE = whole(2, COLS, LEV)
SIDE = whole(3, ROWS, LEV)
BAND = whole(3, COLS, LEV)
ANYWHERE = pl.BlockSpec(memory_space=pl.ANY)


def call(kernel, name, scalars, in_specs, outs, cost, scratch=(), grid=1, vmem=VMEM):
    return pl.pallas_call(
        kernel,
        name=name,
        grid_spec=pltpu.PrefetchScalarGridSpec(
            num_scalar_prefetch=scalars,
            grid=(grid,),
            in_specs=in_specs,
            out_specs=[spec for _, spec in outs],
            scratch_shapes=list(scratch),
        ),
        out_shape=[jax.ShapeDtypeStruct(shape, F32) for shape, _ in outs],
        compiler_params=pltpu.CompilerParams(vmem_limit_bytes=vmem),
        cost_estimate=pl.CostEstimate(flops=cost, bytes_accessed=cost, transcendentals=0),
    )


def moved(x, pairs):
    full = [(lon * LAT + a, lon * LAT + b) for lon in range(LON) for a, b in pairs]
    return lax.ppermute(x, ("lon", "lat"), full)


def body(tables, tracer, wind_u, wind_v, cotangent, cutoff):
    lat = lax.axis_index("lat").astype(jnp.int32).reshape(1)
    ring = [(i, (i + 1) % LON) for i in range(LON)]
    back_ring = [(b, a) for a, b in ring]
    opposite = [(i, (i + LON // 2) % LON) for i in range(LON)]
    tracer, wind_u, wind_v, cotangent = (
        jnp.transpose(f, (1, 0, 2)) for f in (tracer, wind_u, wind_v, cotangent)
    )
    chunks = [((16, SUB, LEV), LINES)] * 3
    slabs = pltpu.VMEM((PAD, WINDOW, LEV), F32)

    first_cols, last_cols, first_rows, last_rows, edge = call(
        borders,
        "borders",
        1,
        [column(0), column(COLS - 1)] * 3 + [FIRST_TILES, LAST_TILES] * 3,
        [((3, ROWS, LEV), SIDE)] * 2 + [((3, COLS, LEV), BAND)] * 2 + [((2, COLS, LEV), EDGE)],
        1_000_000,
        vmem=60 * 1024 * 1024,
    )(
        lat, tracer, tracer, cotangent, cotangent, wind_u, wind_u,
        tracer, tracer, cotangent, cotangent, wind_v, wind_v,
    )
    cot = call(pack_cotangent, "pack_cotangent", 2, [FULL], chunks, 1_000_000, [slabs])(
        lat, cutoff, cotangent
    )
    east = lax.ppermute(first_cols, "lon", back_ring)
    west = lax.ppermute(last_cols, "lon", ring)
    across = lax.ppermute(edge, "lon", opposite)
    down = [(i, i + 1) for i in range(LAT - 1)]
    north = lax.ppermute(last_rows, "lat", down)
    south = lax.ppermute(first_rows, "lat", [(b, a) for a, b in down])
    cot_a, cot_b = moved(cot[1], SPREAD_A), moved(cot[2], SPREAD_B)

    step = call(
        pack_stepped,
        "pack_stepped",
        2,
        [FULL] * 3 + [SIDE, SIDE, EDGE],
        chunks,
        3_000_000,
        [slabs],
    )(lat, cutoff, tracer, wind_u, wind_v, east, west, across)
    step_a, step_b = moved(step[1], SPREAD_A), moved(step[2], SPREAD_B)
    (lines,) = call(
        pick, "pick", 1, [ANYWHERE] * 6, [((32, SUB, LEV), ANYWHERE)], 500_000,
        [pltpu.SemaphoreType.DMA((2,))],
    )(lat, cot[0], cot_a, cot_b, step[0], step_a, step_b)
    lines = lax.all_to_all(lines, "lon", 0, 0, tiled=True)

    low = pl.pallas_call(
        keep_low,
        name="keep_low",
        in_specs=[pl.BlockSpec(memory_space=pltpu.VMEM)] * 5,
        out_shape=jax.ShapeDtypeStruct((LON, SUB, LEV), F32),
        scratch_shapes=[
            pltpu.VMEM((2, MODES, SUB, LEV), F32),
            pltpu.VMEM((2 * PAD, LEV * GROUPS), F32),
        ],
        compiler_params=pltpu.CompilerParams(vmem_limit_bytes=VMEM),
        cost_estimate=pl.CostEstimate(flops=5_000_000, bytes_accessed=3_000_000, transcendentals=0),
    )(lines, *tables)
    back = lax.all_to_all(low, "lon", 0, 0, tiled=True)
    back_a = moved(back, [(b, a) for a, b in SPREAD_A])
    back_b = moved(back, [(b, a) for a, b in SPREAD_B])

    results = call(
        outputs,
        "outputs",
        1,
        [UNITS] * 3 + [FULL] * 4 + [SIDE, SIDE, BAND, BAND, EDGE],
        [((COLS, ROWS, LEV), OUT)] * 4,
        9_000_000,
        [pltpu.VMEM((PAD, ROWS, LEV), F32)] * 2 + [pltpu.VMEM((2, COLS, LEV), F32)] * 2,
        grid=COLS // CHUNK,
    )(
        lat, back, back_a, back_b, tracer, wind_u, wind_v, cotangent, east, west, north, south, across,
    )
    return [jnp.transpose(r, (1, 0, 2)) for r in results]


def solution(mesh):
    field = P("lat", "lon", None)
    tables = tuple(jnp.asarray(t) for t in dft_tables())

    def run(*args):
        return jax.shard_map(
            lambda t, *a: tuple(body(t, *a)),
            mesh=mesh,
            in_specs=(P(), field, field, field, field, P("lat")),
            out_specs=(field,) * 4,
            check_vma=False,
        )(tables, *args)

    return run
```

```python
import functools

import jax
import jax.numpy as jnp
import ml_dtypes
import numpy as np
from jax import lax
from jax.experimental import pallas as pl
from jax.experimental.pallas import tpu as pltpu
from jax.sharding import PartitionSpec as P

F32 = jnp.float32
BF16 = jnp.bfloat16
LON, LAT = 32, 8
ROWS, COLS, LEV = 24, 90, 128
NLON = LON * COLS
POLAR = 12
MODES = LON // 2 + 1
PAD = 96
SUB = PAD // 4
GROUPS = 5
VMEM = 32 * 1024 * 1024
WINDOW = 16
CHUNK = 15

SPREAD_A = ((0, 1), (7, 6))
SPREAD_B = ((0, 3), (7, 4))


def dft_tables():
    place = np.arange(PAD)
    inside = place < COLS
    wave = np.arange(PAD)
    angle = 2 * np.pi * (wave[:, None] * place[None, :] % COLS) / COLS
    live = (wave[:, None] < COLS) & inside[None, :]
    cos, sin = np.where(live, np.cos(angle), 0), np.where(live, np.sin(angle), 0)
    forward = np.block([[cos, sin], [-sin, cos]])

    where = np.where(inside, place, 0)
    where[91] = -1
    where[90] = COLS
    valid = place < COLS + 2
    back_angle = 2 * np.pi * (where[:, None] * wave[None, :] % COLS) / COLS
    back_live = valid[:, None] & (wave[None, :] < COLS)
    bcos, bsin = np.where(back_live, np.cos(back_angle), 0), np.where(back_live, np.sin(back_angle), 0)
    bcos[92, 0] = 1.0
    backward = np.block([[bcos, -bsin], [bsin, bcos]]) / NLON

    def packed(values):
        spread = values.reshape(MODES, 4, SUB).transpose(0, 2, 1)
        return np.repeat(spread, 32, axis=2).astype(np.float32)

    mode = np.arange(MODES)
    turn = 2 * np.pi * (mode[:, None] * np.where(inside, place, 0)[None, :] % NLON) / NLON
    back_turn = 2 * np.pi * (mode[:, None] * where[None, :] % NLON) / NLON
    back_on = np.where(valid[None, :], 1.0, 0.0) * np.ones((MODES, 1))
    back_on[0, 92] = 1.0
    twiddle = np.stack([packed(np.cos(turn)), packed(-np.sin(turn))])
    back_twiddle = np.stack([packed(np.cos(back_turn) * back_on), packed(np.sin(back_turn) * back_on)])

    def split(matrix):
        high = matrix.astype(ml_dtypes.bfloat16)
        low = (matrix - high.astype(np.float64)).astype(ml_dtypes.bfloat16)
        return np.stack([high, low]).astype(np.float32)

    return split(forward), split(backward), twiddle, back_twiddle


def swap_blocks(parts):
    lane = lax.broadcasted_iota(jnp.int32, parts[0].shape, 1)
    low_half, even_block = lane < 64, (lane // 32) % 2 == 0
    first = [None] * 4
    for i in (0, 1):
        a, b = parts[i], parts[i + 2]
        first[i] = jnp.where(low_half, a, pltpu.roll(b, 64, 1))
        first[i + 2] = jnp.where(low_half, pltpu.roll(a, 64, 1), b)
    second = [None] * 4
    for i in (0, 2):
        a, b = first[i], first[i + 1]
        second[i] = jnp.where(even_block, a, pltpu.roll(b, 32, 1))
        second[i + 1] = jnp.where(even_block, pltpu.roll(a, 96, 1), b)
    return second


def start_of(lat):
    return jnp.where(lat[0] == 0, 0, ROWS - POLAR)


def window_of(lat):
    return pl.multiple_of(jnp.where(lat[0] == 0, 0, ROWS - WINDOW), 8)


def line_of(ref, row, count=COLS, first=0):
    rows = ref.shape[1]
    return ref.reshape(ref.shape[0] * rows, LEV)[pl.ds(first * rows + row, count, stride=rows), :]


def shifted(x, above, below):
    rows = x.shape[0]
    place = lax.broadcasted_iota(jnp.int32, x.shape, 0)
    north = jnp.where(place == 0, above, pltpu.roll(x, 1, 0))
    south = jnp.where(place == rows - 1, below, pltpu.roll(x, rows - 1, 0))
    return north, south


def pack_rows(lat, cutoff, slabs, outs):
    first = start_of(lat) - window_of(lat)
    place = lax.broadcasted_iota(jnp.int32, (WINDOW, LEV), 0)
    cuts = jnp.zeros((WINDOW, LEV), F32)
    for k in range(POLAR):
        cuts = jnp.where(place == first + k, cutoff[start_of(lat) + k].astype(F32), cuts)
    slabs[PAD - 2] = jnp.zeros((WINDOW, LEV), F32)
    slabs[PAD - 1] = cuts
    for k in range(POLAR):
        parts = [line_of(slabs, first + k, SUB, SUB * s) for s in range(4)]
        for q, part in enumerate(swap_blocks(parts)):
            outs[k // 4][4 * (k % 4) + q] = part


def pole_row(lat, tr, wv, edge):
    outer = jnp.where(lat[0] == 0, 0, 7)
    edge[0] = line_of(tr, outer)
    edge[1] = line_of(wv, outer)


def pack_cotangent(lat, cutoff, ct, out0, out1, out2, cols, border, slabs):
    rows = pl.ds(window_of(lat), WINDOW)
    for j in range(COLS):
        slabs[j] = ct[j, rows, :]
    for j in range(COLS, PAD - 2):
        slabs[j] = jnp.zeros((WINDOW, LEV), F32)
    pack_rows(lat, cutoff, slabs, (out0, out1, out2))
    cols[0] = ct[0]
    cols[1] = ct[COLS - 1]
    border[0] = line_of(ct, 0)
    border[1] = line_of(ct, ROWS - 1)


def pack_stepped(
    lat, cutoff, tr, wu, wv, ac, ct_cols, ct_rows,
    out0, out1, out2, first_cols, last_cols, first_rows, last_rows, slabs,
):
    rows = pl.ds(window_of(lat), WINDOW)

    def step(j, east, west):
        x = tr[j, rows, :]
        beyond = ac[0, pl.ds(j, 1), :]
        north, south = shifted(x, beyond, beyond)
        slabs[j] = (
            x
            - 0.5 * wu[j, rows, :] * (east - west)
            - 0.5 * wv[j, rows, :] * (north - south)
            + 0.125 * (east + west + north + south - 4.0 * x)
        )

    def middle(i, carry):
        for m in range(8):
            j = 8 * i + m + 1
            step(j, tr[j + 1, rows, :], tr[j - 1, rows, :])
        return carry

    nothing = jnp.zeros((WINDOW, LEV), F32)
    step(0, tr[1, rows, :], nothing)
    lax.fori_loop(0, (COLS - 2) // 8, middle, 0)
    step(COLS - 1, nothing, tr[COLS - 2, rows, :])
    slabs[COLS] = tr[0, rows, :]
    slabs[COLS + 1] = tr[COLS - 1, rows, :]
    slabs[COLS + 2] = 0.125 + 0.5 * wu[0, rows, :]
    slabs[COLS + 3] = 0.125 - 0.5 * wu[COLS - 1, rows, :]
    pack_rows(lat, cutoff, slabs, (out0, out1, out2))
    for i, (j, out) in enumerate(((0, first_cols), (COLS - 1, last_cols))):
        out[0] = tr[j]
        out[1] = ct_cols[i]
        out[2] = wu[j]
    first_rows[0] = line_of(tr, 0)
    last_rows[0] = line_of(tr, ROWS - 1)
    first_rows[1] = (0.125 - 0.5 * line_of(wv, 0)) * ct_rows[0]
    last_rows[1] = (0.125 + 0.5 * line_of(wv, ROWS - 1)) * ct_rows[1]


def times(a, cos, sin):
    if isinstance(sin, float) and sin == 0.0:
        return (a[0] * cos, None if a[1] is None else a[1] * cos) if cos != 1.0 else a
    if a[1] is None:
        return a[0] * cos, a[0] * sin
    return a[0] * cos - a[1] * sin, a[0] * sin + a[1] * cos


def plus(a, b):
    im = b[1] if a[1] is None else (a[1] if b[1] is None else a[1] + b[1])
    return a[0] + b[0], im


def minus(a, b):
    if a[1] is None:
        im = None if b[1] is None else -b[1]
    else:
        im = a[1] if b[1] is None else a[1] - b[1]
    return a[0] - b[0], im


def conj(a):
    return a[0], None if a[1] is None else -a[1]


def quarter(a, sign):
    re, im = a
    return (None if im is None else -sign * im), sign * re


def turned(a, k, n, sign):
    if k == 0:
        return a
    if 4 * k == n:
        re = jnp.zeros_like(a[0]) if a[1] is None else (-a[1] if sign > 0 else a[1])
        return re, (a[0] if sign > 0 else -a[0])
    return times(a, float(np.cos(2 * np.pi * k / n)), float(sign * np.sin(2 * np.pi * k / n)))


def real_dft(values):
    n = len(values)
    if n == 1:
        return [(values[0], None)]
    even, odd = real_dft(values[0::2]), real_dft(values[1::2])
    out = [None] * (n // 2 + 1)
    for k in range(n // 4 + 1):
        t = turned(odd[k], k, n, -1)
        out[k] = plus(even[k], t)
        if n // 2 - k != k:
            out[n // 2 - k] = conj(minus(even[k], t))
    return out


def real_inverse(modes):
    n = 2 * (len(modes) - 1)
    if n == 2:
        return [modes[0][0] + modes[1][0], modes[0][0] - modes[1][0]]
    even, odd = [], []
    for k in range(n // 4 + 1):
        a, b = modes[k], conj(modes[n // 2 - k])
        even.append(plus(a, b))
        odd.append(turned(minus(a, b), k, n, 1))
    out = [None] * n
    out[0::2], out[1::2] = real_inverse(even), real_inverse(odd)
    return out


def three_products(matrix, x):
    high = x.astype(BF16)
    low = (x - high.astype(F32)).astype(BF16)
    dot = functools.partial(jnp.dot, preferred_element_type=F32)
    main, rest = matrix[0].astype(BF16), matrix[1].astype(BF16)
    return dot(main, high) + (dot(main, low) + dot(rest, high))


def pick(lat, own_c, a_c, b_c, own_s, a_s, b_s, out, sems):
    polar = (lat[0] == 0) | (lat[0] == LAT - 1)
    in_a = (lat[0] == 1) | (lat[0] == LAT - 2)

    def copies(c, s):
        return [
            pltpu.make_async_copy(c, out.at[pl.ds(0, 16)], sems.at[0]),
            pltpu.make_async_copy(s, out.at[pl.ds(16, 16)], sems.at[1]),
        ]

    for chosen, c, s in (
        (polar, own_c, own_s),
        (in_a, a_c, a_s),
        (jnp.logical_not(polar | in_a), b_c, b_s),
    ):

        @pl.when(chosen)
        def _():
            for copy in copies(c, s):
                copy.start()

    for copy in copies(own_c, own_s):
        copy.wait()


def keep_low(x, forward, backward, twiddle, back_twiddle, out, lines, rhs, added):
    lane = lax.broadcasted_iota(jnp.int32, (8, LEV), 1)
    spot = lax.broadcasted_iota(jnp.int32, (8, LEV), 0)
    cut = jnp.max(jnp.where((lane >= 96) & (spot == 7), x[0, SUB - 8 : SUB, :], 0.0))
    wide = lax.broadcasted_iota(jnp.int32, (LON, LEV), 1)
    from_west = line_of(x, 20, LON) * pltpu.roll(line_of(x, 19, LON), 1, 0)
    added[0] = jnp.where(wide < 32, pltpu.roll(from_west, 32, 1), 0.0)
    from_east = line_of(x, 21, LON) * pltpu.roll(line_of(x, 18, LON), LON - 1, 0)
    added[1] = jnp.where(wide >= 96, from_east, 0.0)
    for i in range(SUB // 8):
        at = slice(8 * i, 8 * i + 8)
        values = [x[b, at, :] for b in range(LON)]
        if i != 1:
            values = [
                v + jnp.where(spot == i // 2, added[i // 2, b : b + 1, :], 0.0)
                for b, v in enumerate(values)
            ]
        modes = real_dft(values)
        for k, mode in enumerate(modes):
            re, im = times(mode, twiddle[0, k, at, :], twiddle[1, k, at, :])
            lines[0, k, at, :] = re
            lines[1, k, at, :] = im
    zero = jnp.zeros((SUB, LEV), F32)
    for g in range(GROUPS):
        for part in range(2):
            stack = [lines[part, 4 * g + m] if 4 * g + m < MODES else zero for m in range(4)]
            for s, block in enumerate(swap_blocks(stack)):
                rhs[PAD * part + SUB * s : PAD * part + SUB * s + SUB, LEV * g : LEV * g + LEV] = block
    spectrum = three_products(forward, rhs[...])
    shape = (PAD, LEV * GROUPS)
    number = 4 * (lax.broadcasted_iota(jnp.int32, shape, 1) // LEV)
    number = number + (lax.broadcasted_iota(jnp.int32, shape, 1) // 32) % 4
    number = number + 32 * lax.broadcasted_iota(jnp.int32, shape, 0)
    kept = jnp.minimum(number, NLON - number).astype(F32) <= cut
    kept = jnp.concatenate([kept.astype(F32)] * 2, axis=0) > 0.5
    rhs[...] = three_products(backward, jnp.where(kept, spectrum, 0.0))
    for g in range(GROUPS):
        for part in range(2):
            stack = [
                rhs[PAD * part + SUB * s : PAD * part + SUB * s + SUB, LEV * g : LEV * g + LEV]
                for s in range(4)
            ]
            for m, block in enumerate(swap_blocks(stack)):
                if 4 * g + m < MODES:
                    lines[part, 4 * g + m] = block
    for i in range(SUB // 8):
        at = slice(8 * i, 8 * i + 8)
        modes = [
            times(
                (lines[0, k, at, :], lines[1, k, at, :]),
                back_twiddle[0, k, at, :],
                back_twiddle[1, k, at, :],
            )
            for k in range(MODES)
        ]
        for b, value in enumerate(real_inverse(modes)):
            out[b, at, :] = value


def outputs(
    lat, ret0, ret1, ret2, tr, wu, wv, ct, he, hw, n3, s3, ac,
    adv, gt, gu, gv, adjoint, low_stepped, top, bottom, adv_all, gt_all, gu_all, gv_all, sems,
):
    is0, is7 = lat[0] == 0, lat[0] == LAT - 1
    rets = (ret0, ret1, ret2)
    start = start_of(lat)

    def fill(i, carry):
        for m in range(10):
            adjoint[10 * i + m] = ct[10 * i + m]
        return carry

    lax.fori_loop(0, COLS // 10, fill, 0)
    adjoint[COLS] = he[1]
    adjoint[COLS + 1] = hw[1]

    @pl.when(is0 | is7)
    def _():
        flat = adjoint.reshape(PAD * ROWS, LEV)
        flat_stepped = low_stepped.reshape(PAD * ROWS, LEV)
        for k in range(POLAR):
            ret, kk = rets[k // 4], k % 4
            for target, base in ((flat, 0), (flat_stepped, 16)):
                line = swap_blocks([ret[base + 4 * kk + q] for q in range(4)])
                for s, part in enumerate(line):
                    target[pl.ds(SUB * s * ROWS + start + k, SUB, stride=ROWS), :] = part

    outer = jnp.where(is0, 0, ROWS - 1)
    mean = adjoint[COLS + 2, pl.ds(outer, 1), :]
    opposite = 2.0 * mean - line_of(adjoint, outer)
    top[0] = jnp.where(is0, ac[0], n3[0])
    top[1] = jnp.where(is0, (0.125 - 0.5 * ac[1]) * opposite, n3[1])
    bottom[0] = jnp.where(is7, ac[0], s3[0])
    bottom[1] = jnp.where(is7, (0.125 + 0.5 * ac[1]) * opposite, s3[1])

    place = lax.broadcasted_iota(jnp.int32, (ROWS, LEV), 0)
    filtered = (is0 & (place < POLAR)) | (is7 & (place >= ROWS - POLAR))
    results = ((adv_all, adv), (gt_all, gt), (gu_all, gu), (gv_all, gv))

    def sent(step, i):
        block = pl.ds(step * CHUNK, CHUNK)
        return pltpu.make_async_copy(results[i][0].at[block], results[i][1].at[block], sems.at[step, i])

    for j in range(COLS):
        one = slice(j, j + 1)
        x, u, v, a = tr[j], wu[j], wv[j], adjoint[j]
        west, u_west, a_west = (
            (tr[j - 1], wu[j - 1], adjoint[j - 1]) if j else (hw[0], hw[2], adjoint[COLS + 1])
        )
        east, u_east = (tr[j + 1], wu[j + 1]) if j < COLS - 1 else (he[0], he[2])
        a_east = adjoint[j + 1]
        north, south = shifted(x, top[0, one, :], bottom[0, one, :])
        across, along = east - west, north - south
        stepped = (
            x - 0.5 * u * across - 0.5 * v * along + 0.125 * (east + west + north + south - 4.0 * x)
        )
        adv_all[j] = jnp.where(filtered, low_stepped[j], stepped)
        half = -0.5 * a
        gu_all[j] = across * half
        gv_all[j] = along * half
        place_north = jnp.where(
            place == 0, top[1, one, :], pltpu.roll((0.125 + 0.5 * v) * a, 1, 0)
        )
        place_south = jnp.where(
            place == ROWS - 1, bottom[1, one, :], pltpu.roll((0.125 - 0.5 * v) * a, ROWS - 1, 0)
        )
        gt_all[j] = (
            0.5 * a
            + (0.125 + 0.5 * u_east) * a_east
            + (0.125 - 0.5 * u_west) * a_west
            + place_north
            + place_south
        )
        if j % CHUNK == CHUNK - 1:
            for i in range(4):
                sent(j // CHUNK, i).start()
    for step in range(COLS // CHUNK):
        for i in range(4):
            sent(step, i).wait()


def whole(*shape):
    return pl.BlockSpec(shape, lambda i, *m: (0,) * len(shape))


OUTER_TILES = pl.BlockSpec(
    (COLS, 8, LEV), lambda i, lat, *m: (0, jnp.where(lat[0] == 0, 0, ROWS // 8 - 1), 0)
)
EDGE = whole(2, COLS, LEV)
ANYWHERE = pl.BlockSpec(memory_space=pl.ANY)


def call(kernel, name, scalars, in_specs, outs, cost, scratch=(), vmem=VMEM):
    return pl.pallas_call(
        kernel,
        name=name,
        grid_spec=pltpu.PrefetchScalarGridSpec(
            num_scalar_prefetch=scalars,
            grid=(1,),
            in_specs=in_specs,
            out_specs=[spec for _, spec in outs],
            scratch_shapes=list(scratch),
        ),
        out_shape=[jax.ShapeDtypeStruct(shape, F32) for shape, _ in outs],
        compiler_params=pltpu.CompilerParams(vmem_limit_bytes=vmem),
        cost_estimate=pl.CostEstimate(flops=cost, bytes_accessed=cost, transcendentals=0),
    )


def local_call(kernel, name, scalars, inputs, shapes, cost, scratch=(), out_space=pltpu.VMEM):
    return pl.pallas_call(
        kernel,
        name=name,
        in_specs=[pl.BlockSpec(memory_space=pltpu.SMEM)] * scalars
        + [pl.BlockSpec(memory_space=pltpu.VMEM)] * inputs,
        out_specs=[pl.BlockSpec(memory_space=out_space)] * len(shapes),
        scratch_shapes=list(scratch),
        out_shape=[jax.ShapeDtypeStruct(shape, F32) for shape in shapes],
        compiler_params=pltpu.CompilerParams(vmem_limit_bytes=VMEM),
        cost_estimate=pl.CostEstimate(flops=cost, bytes_accessed=cost, transcendentals=0),
    )


def moved(x, pairs):
    full = [(lon * LAT + a, lon * LAT + b) for lon in range(LON) for a, b in pairs]
    return lax.ppermute(x, ("lon", "lat"), full)


def body(tables, tracer, wind_u, wind_v, cotangent, cutoff):
    lat = lax.axis_index("lat").astype(jnp.int32).reshape(1)
    ring = [(i, (i + 1) % LON) for i in range(LON)]
    back_ring = [(b, a) for a, b in ring]
    opposite = [(i, (i + LON // 2) % LON) for i in range(LON)]
    tracer, wind_u, wind_v, cotangent = (
        jnp.transpose(f, (1, 0, 2)) for f in (tracer, wind_u, wind_v, cotangent)
    )
    chunk = (16, SUB, LEV)
    slabs = pltpu.VMEM((PAD, WINDOW, LEV), F32)

    border = ((2, COLS, LEV), EDGE)
    (edge,) = call(
        pole_row, "pole_row", 1, [OUTER_TILES] * 2, [border], 1_000_000, vmem=60 * 1024 * 1024
    )(lat, tracer, wind_v)
    across = lax.ppermute(edge, "lon", opposite)
    *cot, ct_cols, ct_rows = local_call(
        pack_cotangent,
        "pack_cotangent",
        2,
        1,
        [chunk] * 3 + [(2, ROWS, LEV), (2, COLS, LEV)],
        1_000_000,
        [slabs],
    )(lat, cutoff, cotangent)
    cot_a, cot_b = moved(cot[1], SPREAD_A), moved(cot[2], SPREAD_B)

    *step, first_cols, last_cols, first_rows, last_rows = local_call(
        pack_stepped,
        "pack_stepped",
        2,
        6,
        [chunk] * 3 + [(3, ROWS, LEV)] * 2 + [(2, COLS, LEV)] * 2,
        3_000_000,
        [slabs],
    )(lat, cutoff, tracer, wind_u, wind_v, across, ct_cols, ct_rows)
    step_a, step_b = moved(step[1], SPREAD_A), moved(step[2], SPREAD_B)
    east = lax.ppermute(first_cols, "lon", back_ring)
    west = lax.ppermute(last_cols, "lon", ring)
    down = [(i, i + 1) for i in range(LAT - 1)]
    north = lax.ppermute(last_rows, "lat", down)
    south = lax.ppermute(first_rows, "lat", [(b, a) for a, b in down])
    (lines,) = call(
        pick, "pick", 1, [ANYWHERE] * 6, [((32, SUB, LEV), ANYWHERE)], 500_000,
        [pltpu.SemaphoreType.DMA((2,))],
    )(lat, cot[0], cot_a, cot_b, step[0], step_a, step_b)
    lines = lax.all_to_all(lines, "lon", 0, 0, tiled=True)

    low = pl.pallas_call(
        keep_low,
        name="keep_low",
        in_specs=[pl.BlockSpec(memory_space=pltpu.VMEM)] * 5,
        out_shape=jax.ShapeDtypeStruct((LON, SUB, LEV), F32),
        scratch_shapes=[
            pltpu.VMEM((2, MODES, SUB, LEV), F32),
            pltpu.VMEM((2 * PAD, LEV * GROUPS), F32),
            pltpu.VMEM((2, LON, LEV), F32),
        ],
        compiler_params=pltpu.CompilerParams(vmem_limit_bytes=VMEM),
        cost_estimate=pl.CostEstimate(flops=5_000_000, bytes_accessed=3_000_000, transcendentals=0),
    )(lines, *tables)
    back = lax.all_to_all(low, "lon", 0, 0, tiled=True)
    back_a = moved(back, [(b, a) for a, b in SPREAD_A])
    back_b = moved(back, [(b, a) for a, b in SPREAD_B])

    whole_block = (COLS, ROWS, LEV)
    results = local_call(
        outputs,
        "outputs",
        1,
        12,
        [whole_block] * 4,
        9_000_000,
        [pltpu.VMEM((PAD, ROWS, LEV), F32)] * 2
        + [pltpu.VMEM((2, COLS, LEV), F32)] * 2
        + [pltpu.VMEM(whole_block, F32)] * 4
        + [pltpu.SemaphoreType.DMA((COLS // CHUNK, 4))],
        out_space=pl.ANY,
    )(
        lat, back, back_a, back_b, tracer, wind_u, wind_v, cotangent, east, west, north, south, across,
    )
    return [jnp.transpose(r, (1, 0, 2)) for r in results]


def solution(mesh):
    field = P("lat", "lon", None)
    tables = tuple(jnp.asarray(t) for t in dft_tables())

    def run(*args):
        return jax.shard_map(
            lambda t, *a: tuple(body(t, *a)),
            mesh=mesh,
            in_specs=(P(), field, field, field, field, P("lat")),
            out_specs=(field,) * 4,
            check_vma=False,
        )(tables, *args)

    return run
```

```python
import functools

import jax
import jax.numpy as jnp
import ml_dtypes
import numpy as np
from jax import lax
from jax.experimental import pallas as pl
from jax.experimental.pallas import tpu as pltpu
from jax.sharding import PartitionSpec as P

F32 = jnp.float32
BF16 = jnp.bfloat16
LON, LAT = 32, 8
ROWS, COLS, LEV = 24, 90, 128
NLON = LON * COLS
POLAR = 12
MODES = LON // 2 + 1
PAD = 96
SUB = PAD // 4
GROUPS = 5
VMEM = 32 * 1024 * 1024
WINDOW = 16
PITCH = 24
CHUNK = 15

SPREAD_A = ((0, 1), (7, 6))
SPREAD_B = ((0, 3), (7, 4))
EARLY = ((3, 4), (4, 3))
SOUTHWARD = ((0, 1), (1, 2), (2, 3), (4, 5), (5, 6), (6, 7))
NORTHWARD = ((1, 0), (2, 1), (3, 2), (5, 4), (6, 5), (7, 6))


def dft_tables():
    place = np.arange(PAD)
    inside = place < COLS
    wave = np.arange(PAD)
    angle = 2 * np.pi * (wave[:, None] * place[None, :] % COLS) / COLS
    live = (wave[:, None] < COLS) & inside[None, :]
    cos, sin = np.where(live, np.cos(angle), 0), np.where(live, np.sin(angle), 0)
    forward = np.block([[cos, sin], [-sin, cos]])

    where = np.where(inside, place, 0)
    where[91] = -1
    where[90] = COLS
    valid = place < COLS + 2
    back_angle = 2 * np.pi * (where[:, None] * wave[None, :] % COLS) / COLS
    back_live = valid[:, None] & (wave[None, :] < COLS)
    bcos, bsin = np.where(back_live, np.cos(back_angle), 0), np.where(back_live, np.sin(back_angle), 0)
    bcos[92, 0] = 1.0
    backward = np.block([[bcos, -bsin], [bsin, bcos]]) / NLON

    def packed(values):
        spread = values.reshape(MODES, 4, SUB).transpose(0, 2, 1)
        return np.repeat(spread, 32, axis=2).astype(np.float32)

    mode = np.arange(MODES)
    turn = 2 * np.pi * (mode[:, None] * np.where(inside, place, 0)[None, :] % NLON) / NLON
    back_turn = 2 * np.pi * (mode[:, None] * where[None, :] % NLON) / NLON
    back_on = np.where(valid[None, :], 1.0, 0.0) * np.ones((MODES, 1))
    back_on[0, 92] = 1.0
    twiddle = np.stack([packed(np.cos(turn)), packed(-np.sin(turn))])
    back_twiddle = np.stack([packed(np.cos(back_turn) * back_on), packed(np.sin(back_turn) * back_on)])

    def split(matrix):
        high = matrix.astype(ml_dtypes.bfloat16)
        low = (matrix - high.astype(np.float64)).astype(ml_dtypes.bfloat16)
        return np.stack([high, low]).astype(np.float32)

    return split(forward), split(backward), twiddle, back_twiddle


def swap_blocks(parts):
    lane = lax.broadcasted_iota(jnp.int32, parts[0].shape, 1)
    low_half, even_block = lane < 64, (lane // 32) % 2 == 0
    first = [None] * 4
    for i in (0, 1):
        a, b = parts[i], parts[i + 2]
        first[i] = jnp.where(low_half, a, pltpu.roll(b, 64, 1))
        first[i + 2] = jnp.where(low_half, pltpu.roll(a, 64, 1), b)
    second = [None] * 4
    for i in (0, 2):
        a, b = first[i], first[i + 1]
        second[i] = jnp.where(even_block, a, pltpu.roll(b, 32, 1))
        second[i + 1] = jnp.where(even_block, pltpu.roll(a, 96, 1), b)
    return second


def start_of(lat):
    return jnp.where(lat[0] == 0, 0, ROWS - POLAR)


def window_of(lat):
    return pl.multiple_of(jnp.where(lat[0] == 0, 0, ROWS - WINDOW), 8)


def line_of(ref, row, count=COLS, first=0):
    rows = ref.shape[1]
    return ref.reshape(ref.shape[0] * rows, LEV)[pl.ds(first * rows + row, count, stride=rows), :]


def shifted(x, above, below):
    rows = x.shape[0]
    place = lax.broadcasted_iota(jnp.int32, x.shape, 0)
    north = jnp.where(place == 0, above, pltpu.roll(x, 1, 0))
    south = jnp.where(place == rows - 1, below, pltpu.roll(x, rows - 1, 0))
    return north, south


def pack_rows(lat, cutoff, slabs, outs):
    first = start_of(lat) - window_of(lat)
    place = lax.broadcasted_iota(jnp.int32, (WINDOW, LEV), 0)
    cuts = jnp.zeros((WINDOW, LEV), F32)
    for k in range(POLAR):
        cuts = jnp.where(place == first + k, cutoff[start_of(lat) + k].astype(F32), cuts)
    slabs[PAD - 2, 0:WINDOW, :] = jnp.zeros((WINDOW, LEV), F32)
    slabs[PAD - 1, 0:WINDOW, :] = cuts
    for k in range(POLAR):
        parts = [line_of(slabs, first + k, SUB, SUB * s) for s in range(4)]
        for q, part in enumerate(swap_blocks(parts)):
            outs[k // 4][4 * (k % 4) + q] = part


def pole_row(lat, tr, wv, edge):
    outer = jnp.where(lat[0] == 0, 0, 7)
    edge[0] = line_of(tr, outer)
    edge[1] = line_of(wv, outer)


def pack_cotangent(lat, cutoff, ct, out0, out1, out2, cols, border, slabs):
    rows = pl.ds(window_of(lat), WINDOW)
    for j in range(COLS):
        slabs[j, 0:WINDOW, :] = ct[j, rows, :]
    for j in range(COLS, PAD - 2):
        slabs[j, 0:WINDOW, :] = jnp.zeros((WINDOW, LEV), F32)
    pack_rows(lat, cutoff, slabs, (out0, out1, out2))
    cols[0] = ct[0]
    cols[1] = ct[COLS - 1]
    border[0] = line_of(ct, 0)
    border[1] = line_of(ct, ROWS - 1)


def pack_stepped(
    lat, cutoff, tr, wu, wv, ac, ct_cols, ct_rows,
    out0, out1, out2, first_cols, last_cols, first_rows, last_rows, early_rows, slabs,
):
    rows = pl.ds(window_of(lat), WINDOW)

    def step(j, east, west):
        x = tr[j, rows, :]
        beyond = ac[0, pl.ds(j, 1), :]
        north, south = shifted(x, beyond, beyond)
        slabs[j, 0:WINDOW, :] = (
            x
            - 0.5 * wu[j, rows, :] * (east - west)
            - 0.5 * wv[j, rows, :] * (north - south)
            + 0.125 * (east + west + north + south - 4.0 * x)
        )

    def middle(i, carry):
        for m in range(8):
            j = 8 * i + m + 1
            step(j, tr[j + 1, rows, :], tr[j - 1, rows, :])
        return carry

    nothing = jnp.zeros((WINDOW, LEV), F32)
    step(0, tr[1, rows, :], nothing)
    lax.fori_loop(0, (COLS - 2) // 8, middle, 0)
    step(COLS - 1, nothing, tr[COLS - 2, rows, :])
    slabs[COLS, 0:WINDOW, :] = tr[0, rows, :]
    slabs[COLS + 1, 0:WINDOW, :] = tr[COLS - 1, rows, :]
    slabs[COLS + 2, 0:WINDOW, :] = 0.125 + 0.5 * wu[0, rows, :]
    slabs[COLS + 3, 0:WINDOW, :] = 0.125 - 0.5 * wu[COLS - 1, rows, :]
    pack_rows(lat, cutoff, slabs, (out0, out1, out2))
    for i, (j, out) in enumerate(((0, first_cols), (COLS - 1, last_cols))):
        out[0] = tr[j]
        out[1] = ct_cols[i]
        out[2] = wu[j]
    first_rows[0] = line_of(tr, 0)
    last_rows[0] = line_of(tr, ROWS - 1)
    first_rows[1] = (0.125 - 0.5 * line_of(wv, 0)) * ct_rows[0]
    last_rows[1] = (0.125 + 0.5 * line_of(wv, ROWS - 1)) * ct_rows[1]
    for i in range(2):
        early_rows[i] = jnp.where(lat[0] == 3, last_rows[i], first_rows[i])


def times(a, cos, sin):
    if isinstance(sin, float) and sin == 0.0:
        return (a[0] * cos, None if a[1] is None else a[1] * cos) if cos != 1.0 else a
    if a[1] is None:
        return a[0] * cos, a[0] * sin
    return a[0] * cos - a[1] * sin, a[0] * sin + a[1] * cos


def plus(a, b):
    im = b[1] if a[1] is None else (a[1] if b[1] is None else a[1] + b[1])
    return a[0] + b[0], im


def minus(a, b):
    if a[1] is None:
        im = None if b[1] is None else -b[1]
    else:
        im = a[1] if b[1] is None else a[1] - b[1]
    return a[0] - b[0], im


def conj(a):
    return a[0], None if a[1] is None else -a[1]


def quarter(a, sign):
    re, im = a
    return (None if im is None else -sign * im), sign * re


def turned(a, k, n, sign):
    if k == 0:
        return a
    if 4 * k == n:
        re = jnp.zeros_like(a[0]) if a[1] is None else (-a[1] if sign > 0 else a[1])
        return re, (a[0] if sign > 0 else -a[0])
    return times(a, float(np.cos(2 * np.pi * k / n)), float(sign * np.sin(2 * np.pi * k / n)))


def real_dft(values):
    n = len(values)
    if n == 1:
        return [(values[0], None)]
    even, odd = real_dft(values[0::2]), real_dft(values[1::2])
    out = [None] * (n // 2 + 1)
    for k in range(n // 4 + 1):
        t = turned(odd[k], k, n, -1)
        out[k] = plus(even[k], t)
        if n // 2 - k != k:
            out[n // 2 - k] = conj(minus(even[k], t))
    return out


def real_inverse(modes):
    n = 2 * (len(modes) - 1)
    if n == 2:
        return [modes[0][0] + modes[1][0], modes[0][0] - modes[1][0]]
    even, odd = [], []
    for k in range(n // 4 + 1):
        a, b = modes[k], conj(modes[n // 2 - k])
        even.append(plus(a, b))
        odd.append(turned(minus(a, b), k, n, 1))
    out = [None] * n
    out[0::2], out[1::2] = real_inverse(even), real_inverse(odd)
    return out


def three_products(matrix, x):
    high = x.astype(BF16)
    low = (x - high.astype(F32)).astype(BF16)
    dot = functools.partial(jnp.dot, preferred_element_type=F32)
    main, rest = matrix[0].astype(BF16), matrix[1].astype(BF16)
    return dot(main, high) + (dot(main, low) + dot(rest, high))


def pick(lat, own_c, a_c, b_c, own_s, a_s, b_s, early, out, sems):
    polar = (lat[0] == 0) | (lat[0] == LAT - 1)
    in_a = (lat[0] == 1) | (lat[0] == LAT - 2)

    def copies(c, s):
        return [
            pltpu.make_async_copy(c, out.at[pl.ds(0, 16)], sems.at[0]),
            pltpu.make_async_copy(s, out.at[pl.ds(16, 16)], sems.at[1]),
        ]

    for chosen, c, s in (
        (polar, own_c, own_s),
        (in_a, a_c, a_s),
        (jnp.logical_not(polar | in_a), b_c, b_s),
    ):

        @pl.when(chosen)
        def _():
            for copy in copies(c, s):
                copy.start()

    for copy in copies(own_c, own_s):
        copy.wait()


def keep_low(x, forward, backward, twiddle, back_twiddle, out, lines, rhs, added):
    lane = lax.broadcasted_iota(jnp.int32, (8, LEV), 1)
    spot = lax.broadcasted_iota(jnp.int32, (8, LEV), 0)
    cut = jnp.max(jnp.where((lane >= 96) & (spot == 7), x[0, SUB - 8 : SUB, :], 0.0))
    wide = lax.broadcasted_iota(jnp.int32, (LON, LEV), 1)
    from_west = line_of(x, 20, LON) * pltpu.roll(line_of(x, 19, LON), 1, 0)
    added[0] = jnp.where(wide < 32, pltpu.roll(from_west, 32, 1), 0.0)
    from_east = line_of(x, 21, LON) * pltpu.roll(line_of(x, 18, LON), LON - 1, 0)
    added[1] = jnp.where(wide >= 96, from_east, 0.0)
    for i in range(SUB // 8):
        at = slice(8 * i, 8 * i + 8)
        values = [x[b, at, :] for b in range(LON)]
        if i != 1:
            values = [
                v + jnp.where(spot == i // 2, added[i // 2, b : b + 1, :], 0.0)
                for b, v in enumerate(values)
            ]
        modes = real_dft(values)
        for k, mode in enumerate(modes):
            re, im = times(mode, twiddle[0, k, at, :], twiddle[1, k, at, :])
            lines[0, k, at, :] = re
            lines[1, k, at, :] = im
    zero = jnp.zeros((SUB, LEV), F32)
    for g in range(GROUPS):
        for part in range(2):
            stack = [lines[part, 4 * g + m] if 4 * g + m < MODES else zero for m in range(4)]
            for s, block in enumerate(swap_blocks(stack)):
                rhs[PAD * part + SUB * s : PAD * part + SUB * s + SUB, LEV * g : LEV * g + LEV] = block
    spectrum = three_products(forward, rhs[...])
    shape = (PAD, LEV * GROUPS)
    number = 4 * (lax.broadcasted_iota(jnp.int32, shape, 1) // LEV)
    number = number + (lax.broadcasted_iota(jnp.int32, shape, 1) // 32) % 4
    number = number + 32 * lax.broadcasted_iota(jnp.int32, shape, 0)
    kept = jnp.minimum(number, NLON - number).astype(F32) <= cut
    kept = jnp.concatenate([kept.astype(F32)] * 2, axis=0) > 0.5
    rhs[...] = three_products(backward, jnp.where(kept, spectrum, 0.0))
    for g in range(GROUPS):
        for part in range(2):
            stack = [
                rhs[PAD * part + SUB * s : PAD * part + SUB * s + SUB, LEV * g : LEV * g + LEV]
                for s in range(4)
            ]
            for m, block in enumerate(swap_blocks(stack)):
                if 4 * g + m < MODES:
                    lines[part, 4 * g + m] = block
    for i in range(SUB // 8):
        at = slice(8 * i, 8 * i + 8)
        modes = [
            times(
                (lines[0, k, at, :], lines[1, k, at, :]),
                back_twiddle[0, k, at, :],
                back_twiddle[1, k, at, :],
            )
            for k in range(MODES)
        ]
        for b, value in enumerate(real_inverse(modes)):
            out[b, at, :] = value


def outputs(
    lat, ret0, ret1, ret2, tr, wu, wv, ct, he, hw, n3, s3, early, ac,
    adv, gt, gu, gv, adjoint, low_stepped, top, bottom, adv_all, gt_all, gu_all, gv_all, sems,
):
    is0, is7 = lat[0] == 0, lat[0] == LAT - 1
    rets = (ret0, ret1, ret2)
    start = start_of(lat)

    def fill(i, carry):
        for m in range(10):
            adjoint[10 * i + m] = ct[10 * i + m]
        return carry

    lax.fori_loop(0, COLS // 10, fill, 0)
    adjoint[COLS] = he[1]
    adjoint[COLS + 1] = hw[1]

    @pl.when(is0 | is7)
    def _():
        flat = adjoint.reshape(PAD * ROWS, LEV)
        flat_stepped = low_stepped.reshape(PAD * ROWS, LEV)
        for k in range(POLAR):
            ret, kk = rets[k // 4], k % 4
            for target, base in ((flat, 0), (flat_stepped, 16)):
                line = swap_blocks([ret[base + 4 * kk + q] for q in range(4)])
                for s, part in enumerate(line):
                    target[pl.ds(SUB * s * ROWS + start + k, SUB, stride=ROWS), :] = part

    outer = jnp.where(is0, 0, ROWS - 1)
    mean = adjoint[COLS + 2, pl.ds(outer, 1), :]
    opposite = 2.0 * mean - line_of(adjoint, outer)
    early_north, early_south = lat[0] == 4, lat[0] == 3
    tr_north, north = (jnp.where(early_north, early[i], n3[i]) for i in range(2))
    tr_south, south = (jnp.where(early_south, early[i], s3[i]) for i in range(2))
    top[0] = jnp.where(is0, ac[0], tr_north)
    top[1] = jnp.where(is0, (0.125 - 0.5 * ac[1]) * opposite, north)
    bottom[0] = jnp.where(is7, ac[0], tr_south)
    bottom[1] = jnp.where(is7, (0.125 + 0.5 * ac[1]) * opposite, south)

    place = lax.broadcasted_iota(jnp.int32, (ROWS, LEV), 0)
    filtered = (is0 & (place < POLAR)) | (is7 & (place >= ROWS - POLAR))
    results = ((adv_all, adv), (gt_all, gt), (gu_all, gu), (gv_all, gv))

    def sent(step, i):
        block = pl.ds(step * CHUNK, CHUNK)
        return pltpu.make_async_copy(results[i][0].at[block], results[i][1].at[block], sems.at[step, i])

    for j in range(COLS):
        one = slice(j, j + 1)
        x, u, v, a = tr[j], wu[j], wv[j], adjoint[j]
        west, u_west, a_west = (
            (tr[j - 1], wu[j - 1], adjoint[j - 1]) if j else (hw[0], hw[2], adjoint[COLS + 1])
        )
        east, u_east = (tr[j + 1], wu[j + 1]) if j < COLS - 1 else (he[0], he[2])
        a_east = adjoint[j + 1]
        north, south = shifted(x, top[0, one, :], bottom[0, one, :])
        across, along = east - west, north - south
        stepped = (
            x - 0.5 * u * across - 0.5 * v * along + 0.125 * (east + west + north + south - 4.0 * x)
        )
        adv_all[j] = jnp.where(filtered, low_stepped[j], stepped)
        half = -0.5 * a
        gu_all[j] = across * half
        gv_all[j] = along * half
        place_north = jnp.where(
            place == 0, top[1, one, :], pltpu.roll((0.125 + 0.5 * v) * a, 1, 0)
        )
        place_south = jnp.where(
            place == ROWS - 1, bottom[1, one, :], pltpu.roll((0.125 - 0.5 * v) * a, ROWS - 1, 0)
        )
        gt_all[j] = (
            0.5 * a
            + (0.125 + 0.5 * u_east) * a_east
            + (0.125 - 0.5 * u_west) * a_west
            + place_north
            + place_south
        )
        if j % CHUNK == CHUNK - 1:
            for i in range(4):
                sent(j // CHUNK, i).start()
    for step in range(COLS // CHUNK):
        for i in range(4):
            sent(step, i).wait()


def whole(*shape):
    return pl.BlockSpec(shape, lambda i, *m: (0,) * len(shape))


OUTER_TILES = pl.BlockSpec(
    (COLS, 8, LEV), lambda i, lat, *m: (0, jnp.where(lat[0] == 0, 0, ROWS // 8 - 1), 0)
)
EDGE = whole(2, COLS, LEV)
ANYWHERE = pl.BlockSpec(memory_space=pl.ANY)


def call(kernel, name, scalars, in_specs, outs, cost, scratch=(), vmem=VMEM):
    return pl.pallas_call(
        kernel,
        name=name,
        grid_spec=pltpu.PrefetchScalarGridSpec(
            num_scalar_prefetch=scalars,
            grid=(1,),
            in_specs=in_specs,
            out_specs=[spec for _, spec in outs],
            scratch_shapes=list(scratch),
        ),
        out_shape=[jax.ShapeDtypeStruct(shape, F32) for shape, _ in outs],
        compiler_params=pltpu.CompilerParams(vmem_limit_bytes=vmem),
        cost_estimate=pl.CostEstimate(flops=cost, bytes_accessed=cost, transcendentals=0),
    )


def local_call(kernel, name, scalars, inputs, shapes, cost, scratch=(), out_space=pltpu.VMEM):
    return pl.pallas_call(
        kernel,
        name=name,
        in_specs=[pl.BlockSpec(memory_space=pltpu.SMEM)] * scalars
        + [pl.BlockSpec(memory_space=pltpu.VMEM)] * inputs,
        out_specs=[pl.BlockSpec(memory_space=out_space)] * len(shapes),
        scratch_shapes=list(scratch),
        out_shape=[jax.ShapeDtypeStruct(shape, F32) for shape in shapes],
        compiler_params=pltpu.CompilerParams(vmem_limit_bytes=VMEM),
        cost_estimate=pl.CostEstimate(flops=cost, bytes_accessed=cost, transcendentals=0),
    )


def moved(x, pairs):
    full = [(lon * LAT + a, lon * LAT + b) for lon in range(LON) for a, b in pairs]
    return lax.ppermute(x, ("lon", "lat"), full)


def body(tables, tracer, wind_u, wind_v, cotangent, cutoff):
    lat = lax.axis_index("lat").astype(jnp.int32).reshape(1)
    ring = [(i, (i + 1) % LON) for i in range(LON)]
    back_ring = [(b, a) for a, b in ring]
    opposite = [(i, (i + LON // 2) % LON) for i in range(LON)]
    tracer, wind_u, wind_v, cotangent = (
        jnp.transpose(f, (1, 0, 2)) for f in (tracer, wind_u, wind_v, cotangent)
    )
    chunk = (16, SUB, LEV)
    slabs = pltpu.VMEM((PAD, PITCH, LEV), F32)

    border = ((2, COLS, LEV), EDGE)
    (edge,) = call(
        pole_row, "pole_row", 1, [OUTER_TILES] * 2, [border], 1_000_000, vmem=60 * 1024 * 1024
    )(lat, tracer, wind_v)
    across = lax.ppermute(edge, "lon", opposite)
    *cot, ct_cols, ct_rows = local_call(
        pack_cotangent,
        "pack_cotangent",
        2,
        1,
        [chunk] * 3 + [(2, ROWS, LEV), (2, COLS, LEV)],
        1_000_000,
        [slabs],
    )(lat, cutoff, cotangent)
    cot_a, cot_b = moved(cot[1], SPREAD_A), moved(cot[2], SPREAD_B)

    *step, first_cols, last_cols, first_rows, last_rows, early_rows = local_call(
        pack_stepped,
        "pack_stepped",
        2,
        6,
        [chunk] * 3 + [(3, ROWS, LEV)] * 2 + [(2, COLS, LEV)] * 3,
        3_000_000,
        [slabs],
    )(lat, cutoff, tracer, wind_u, wind_v, across, ct_cols, ct_rows)
    step_a, step_b = moved(step[1], SPREAD_A), moved(step[2], SPREAD_B)
    east = lax.ppermute(first_cols, "lon", back_ring)
    west = lax.ppermute(last_cols, "lon", ring)
    early = moved(early_rows, EARLY)
    north, south = moved(last_rows, SOUTHWARD), moved(first_rows, NORTHWARD)
    (lines,) = call(
        pick, "pick", 1, [ANYWHERE] * 7, [((32, SUB, LEV), ANYWHERE)], 500_000,
        [pltpu.SemaphoreType.DMA((2,))],
    )(lat, cot[0], cot_a, cot_b, step[0], step_a, step_b, early)
    lines = lax.all_to_all(lines, "lon", 0, 0, tiled=True)

    low = pl.pallas_call(
        keep_low,
        name="keep_low",
        in_specs=[pl.BlockSpec(memory_space=pltpu.VMEM)] * 5,
        out_shape=jax.ShapeDtypeStruct((LON, SUB, LEV), F32),
        scratch_shapes=[
            pltpu.VMEM((2, MODES, SUB, LEV), F32),
            pltpu.VMEM((2 * PAD, LEV * GROUPS), F32),
            pltpu.VMEM((2, LON, LEV), F32),
        ],
        compiler_params=pltpu.CompilerParams(vmem_limit_bytes=VMEM),
        cost_estimate=pl.CostEstimate(flops=5_000_000, bytes_accessed=3_000_000, transcendentals=0),
    )(lines, *tables)
    back = lax.all_to_all(low, "lon", 0, 0, tiled=True)
    back_a = moved(back, [(b, a) for a, b in SPREAD_A])
    back_b = moved(back, [(b, a) for a, b in SPREAD_B])

    whole_block = (COLS, ROWS, LEV)
    results = local_call(
        outputs,
        "outputs",
        1,
        13,
        [whole_block] * 4,
        9_000_000,
        [pltpu.VMEM((PAD, ROWS, LEV), F32)] * 2
        + [pltpu.VMEM((2, COLS, LEV), F32)] * 2
        + [pltpu.VMEM(whole_block, F32)] * 4
        + [pltpu.SemaphoreType.DMA((COLS // CHUNK, 4))],
        out_space=pl.ANY,
    )(
        lat, back, back_a, back_b, tracer, wind_u, wind_v, cotangent, east, west, north, south,
        early, across,
    )
    return [jnp.transpose(r, (1, 0, 2)) for r in results]


def solution(mesh):
    field = P("lat", "lon", None)
    tables = tuple(jnp.asarray(t) for t in dft_tables())

    def run(*args):
        return jax.shard_map(
            lambda t, *a: tuple(body(t, *a)),
            mesh=mesh,
            in_specs=(P(), field, field, field, field, P("lat")),
            out_specs=(field,) * 4,
            check_vma=False,
        )(tables, *args)

    return run
```

```python
import functools

import jax
import jax.numpy as jnp
import ml_dtypes
import numpy as np
from jax import lax
from jax.experimental import pallas as pl
from jax.experimental.pallas import tpu as pltpu
from jax.sharding import PartitionSpec as P

F32 = jnp.float32
BF16 = jnp.bfloat16
LON, LAT = 32, 8
ROWS, COLS, LEV = 24, 90, 128
NLON = LON * COLS
POLAR = 12
MODES = LON // 2 + 1
PAD = 96
SUB = PAD // 4
GROUPS = 5
VMEM = 32 * 1024 * 1024
WINDOW = 16
PITCH = 24
CHUNK = 15

SPREAD_A = ((0, 1), (7, 6))
SPREAD_B = ((0, 3), (7, 4))
EARLY = ((3, 4), (4, 3))
SOUTHWARD = ((0, 1), (1, 2), (2, 3), (4, 5), (5, 6), (6, 7))
NORTHWARD = ((1, 0), (2, 1), (3, 2), (5, 4), (6, 5), (7, 6))


def dft_tables():
    place = np.arange(PAD)
    inside = place < COLS
    wave = np.arange(PAD)
    angle = 2 * np.pi * (wave[:, None] * place[None, :] % COLS) / COLS
    live = (wave[:, None] < COLS) & inside[None, :]
    cos, sin = np.where(live, np.cos(angle), 0), np.where(live, np.sin(angle), 0)
    forward = np.block([[cos, sin], [-sin, cos]])

    where = np.where(inside, place, 0)
    where[91] = -1
    where[90] = COLS
    valid = place < COLS + 2
    back_angle = 2 * np.pi * (where[:, None] * wave[None, :] % COLS) / COLS
    back_live = valid[:, None] & (wave[None, :] < COLS)
    bcos, bsin = np.where(back_live, np.cos(back_angle), 0), np.where(back_live, np.sin(back_angle), 0)
    bcos[92, 0] = 1.0
    backward = np.block([[bcos, -bsin], [bsin, bcos]]) / NLON

    def packed(values):
        spread = values.reshape(MODES, 4, SUB).transpose(0, 2, 1)
        return np.repeat(spread, 32, axis=2).astype(np.float32)

    mode = np.arange(MODES)
    turn = 2 * np.pi * (mode[:, None] * np.where(inside, place, 0)[None, :] % NLON) / NLON
    back_turn = 2 * np.pi * (mode[:, None] * where[None, :] % NLON) / NLON
    back_on = np.where(valid[None, :], 1.0, 0.0) * np.ones((MODES, 1))
    back_on[0, 92] = 1.0
    twiddle = np.stack([packed(np.cos(turn)), packed(-np.sin(turn))])
    back_twiddle = np.stack([packed(np.cos(back_turn) * back_on), packed(np.sin(back_turn) * back_on)])

    def split(matrix):
        high = matrix.astype(ml_dtypes.bfloat16)
        low = (matrix - high.astype(np.float64)).astype(ml_dtypes.bfloat16)
        return np.stack([high, low]).astype(np.float32)

    return split(forward), split(backward), twiddle, back_twiddle


def swap_blocks(parts):
    lane = lax.broadcasted_iota(jnp.int32, parts[0].shape, 1)
    low_half, even_block = lane < 64, (lane // 32) % 2 == 0
    first = [None] * 4
    for i in (0, 1):
        a, b = parts[i], parts[i + 2]
        first[i] = jnp.where(low_half, a, pltpu.roll(b, 64, 1))
        first[i + 2] = jnp.where(low_half, pltpu.roll(a, 64, 1), b)
    second = [None] * 4
    for i in (0, 2):
        a, b = first[i], first[i + 1]
        second[i] = jnp.where(even_block, a, pltpu.roll(b, 32, 1))
        second[i + 1] = jnp.where(even_block, pltpu.roll(a, 96, 1), b)
    return second


def start_of(lat):
    return jnp.where(lat[0] == 0, 0, ROWS - POLAR)


def window_of(lat):
    return pl.multiple_of(jnp.where(lat[0] == 0, 0, ROWS - WINDOW), 8)


def line_of(ref, row, count=COLS, first=0):
    rows = ref.shape[1]
    flat = ref.reshape(ref.shape[0] * rows, LEV)
    start, whole_tiles = first * rows + row, count // 8 * 8
    line = flat[pl.ds(start, whole_tiles, stride=rows), :]
    rest = [flat[pl.ds(start + j * rows, 1), :] for j in range(whole_tiles, count)]
    return jnp.concatenate([line] + rest, axis=0) if rest else line


def shifted(x, above, below):
    rows = x.shape[0]
    place = lax.broadcasted_iota(jnp.int32, x.shape, 0)
    north = jnp.where(place == 0, above, pltpu.roll(x, 1, 0))
    south = jnp.where(place == rows - 1, below, pltpu.roll(x, rows - 1, 0))
    return north, south


def pack_rows(lat, cutoff, slabs, outs):
    first = start_of(lat) - window_of(lat)
    place = lax.broadcasted_iota(jnp.int32, (WINDOW, LEV), 0)
    cuts = jnp.zeros((WINDOW, LEV), F32)
    for k in range(POLAR):
        cuts = jnp.where(place == first + k, cutoff[start_of(lat) + k].astype(F32), cuts)
    slabs[PAD - 2, 0:WINDOW, :] = jnp.zeros((WINDOW, LEV), F32)
    slabs[PAD - 1, 0:WINDOW, :] = cuts
    for k in range(POLAR):
        parts = [line_of(slabs, first + k, SUB, SUB * s) for s in range(4)]
        for q, part in enumerate(swap_blocks(parts)):
            outs[k // 4][4 * (k % 4) + q] = part


def pole_row(lat, tr, wv, edge):
    outer = jnp.where(lat[0] == 0, 0, 7)
    edge[0] = line_of(tr, outer)
    edge[1] = line_of(wv, outer)


def pack_cotangent(lat, cutoff, ct, out0, out1, out2, cols, border, slabs):
    rows = pl.ds(window_of(lat), WINDOW)
    for j in range(COLS):
        slabs[j, 0:WINDOW, :] = ct[j, rows, :]
    for j in range(COLS, PAD - 2):
        slabs[j, 0:WINDOW, :] = jnp.zeros((WINDOW, LEV), F32)
    pack_rows(lat, cutoff, slabs, (out0, out1, out2))
    cols[0] = ct[0]
    cols[1] = ct[COLS - 1]
    border[0] = line_of(ct, 0)
    border[1] = line_of(ct, ROWS - 1)


def pack_stepped(
    lat, cutoff, tr, wu, wv, ac, ct_cols, ct_rows,
    out0, out1, out2, first_cols, last_cols, first_rows, last_rows, early_rows, slabs,
):
    rows = pl.ds(window_of(lat), WINDOW)

    def step(j, east, west):
        x = tr[j, rows, :]
        beyond = ac[0, pl.ds(j, 1), :]
        north, south = shifted(x, beyond, beyond)
        slabs[j, 0:WINDOW, :] = (
            x
            - 0.5 * wu[j, rows, :] * (east - west)
            - 0.5 * wv[j, rows, :] * (north - south)
            + 0.125 * (east + west + north + south - 4.0 * x)
        )

    def middle(i, carry):
        for m in range(8):
            j = 8 * i + m + 1
            step(j, tr[j + 1, rows, :], tr[j - 1, rows, :])
        return carry

    nothing = jnp.zeros((WINDOW, LEV), F32)
    step(0, tr[1, rows, :], nothing)
    lax.fori_loop(0, (COLS - 2) // 8, middle, 0)
    step(COLS - 1, nothing, tr[COLS - 2, rows, :])
    slabs[COLS, 0:WINDOW, :] = tr[0, rows, :]
    slabs[COLS + 1, 0:WINDOW, :] = tr[COLS - 1, rows, :]
    slabs[COLS + 2, 0:WINDOW, :] = 0.125 + 0.5 * wu[0, rows, :]
    slabs[COLS + 3, 0:WINDOW, :] = 0.125 - 0.5 * wu[COLS - 1, rows, :]
    pack_rows(lat, cutoff, slabs, (out0, out1, out2))
    for i, (j, out) in enumerate(((0, first_cols), (COLS - 1, last_cols))):
        out[0] = tr[j]
        out[1] = ct_cols[i]
        out[2] = wu[j]
    first_rows[0] = line_of(tr, 0)
    last_rows[0] = line_of(tr, ROWS - 1)
    first_rows[1] = (0.125 - 0.5 * line_of(wv, 0)) * ct_rows[0]
    last_rows[1] = (0.125 + 0.5 * line_of(wv, ROWS - 1)) * ct_rows[1]
    for i in range(2):
        early_rows[i] = jnp.where(lat[0] == 3, last_rows[i], first_rows[i])


def times(a, cos, sin):
    if isinstance(sin, float) and sin == 0.0:
        return (a[0] * cos, None if a[1] is None else a[1] * cos) if cos != 1.0 else a
    if a[1] is None:
        return a[0] * cos, a[0] * sin
    return a[0] * cos - a[1] * sin, a[0] * sin + a[1] * cos


def plus(a, b):
    im = b[1] if a[1] is None else (a[1] if b[1] is None else a[1] + b[1])
    return a[0] + b[0], im


def minus(a, b):
    if a[1] is None:
        im = None if b[1] is None else -b[1]
    else:
        im = a[1] if b[1] is None else a[1] - b[1]
    return a[0] - b[0], im


def conj(a):
    return a[0], None if a[1] is None else -a[1]


def quarter(a, sign):
    re, im = a
    return (None if im is None else -sign * im), sign * re


def turned(a, k, n, sign):
    if k == 0:
        return a
    if 4 * k == n:
        re = jnp.zeros_like(a[0]) if a[1] is None else (-a[1] if sign > 0 else a[1])
        return re, (a[0] if sign > 0 else -a[0])
    return times(a, float(np.cos(2 * np.pi * k / n)), float(sign * np.sin(2 * np.pi * k / n)))


def real_dft(values):
    n = len(values)
    if n == 1:
        return [(values[0], None)]
    even, odd = real_dft(values[0::2]), real_dft(values[1::2])
    out = [None] * (n // 2 + 1)
    for k in range(n // 4 + 1):
        t = turned(odd[k], k, n, -1)
        out[k] = plus(even[k], t)
        if n // 2 - k != k:
            out[n // 2 - k] = conj(minus(even[k], t))
    return out


def real_inverse(modes):
    n = 2 * (len(modes) - 1)
    if n == 2:
        return [modes[0][0] + modes[1][0], modes[0][0] - modes[1][0]]
    even, odd = [], []
    for k in range(n // 4 + 1):
        a, b = modes[k], conj(modes[n // 2 - k])
        even.append(plus(a, b))
        odd.append(turned(minus(a, b), k, n, 1))
    out = [None] * n
    out[0::2], out[1::2] = real_inverse(even), real_inverse(odd)
    return out


def three_products(matrix, x):
    high = x.astype(BF16)
    low = (x - high.astype(F32)).astype(BF16)
    dot = functools.partial(jnp.dot, preferred_element_type=F32)
    main, rest = matrix[0].astype(BF16), matrix[1].astype(BF16)
    return dot(main, high) + (dot(main, low) + dot(rest, high))


def pick(lat, own_c, a_c, b_c, own_s, a_s, b_s, early, out, sems):
    polar = (lat[0] == 0) | (lat[0] == LAT - 1)
    in_a = (lat[0] == 1) | (lat[0] == LAT - 2)

    def copies(c, s):
        return [
            pltpu.make_async_copy(c, out.at[pl.ds(0, 16)], sems.at[0]),
            pltpu.make_async_copy(s, out.at[pl.ds(16, 16)], sems.at[1]),
        ]

    for chosen, c, s in (
        (polar, own_c, own_s),
        (in_a, a_c, a_s),
        (jnp.logical_not(polar | in_a), b_c, b_s),
    ):

        @pl.when(chosen)
        def _():
            for copy in copies(c, s):
                copy.start()

    for copy in copies(own_c, own_s):
        copy.wait()


def keep_low(x, forward, backward, twiddle, back_twiddle, out, lines, rhs, added):
    lane = lax.broadcasted_iota(jnp.int32, (8, LEV), 1)
    spot = lax.broadcasted_iota(jnp.int32, (8, LEV), 0)
    cut = jnp.max(jnp.where((lane >= 96) & (spot == 7), x[0, SUB - 8 : SUB, :], 0.0))
    wide = lax.broadcasted_iota(jnp.int32, (LON, LEV), 1)
    from_west = line_of(x, 20, LON) * pltpu.roll(line_of(x, 19, LON), 1, 0)
    added[0] = jnp.where(wide < 32, pltpu.roll(from_west, 32, 1), 0.0)
    from_east = line_of(x, 21, LON) * pltpu.roll(line_of(x, 18, LON), LON - 1, 0)
    added[1] = jnp.where(wide >= 96, from_east, 0.0)
    for i in range(SUB // 8):
        at = slice(8 * i, 8 * i + 8)
        values = [x[b, at, :] for b in range(LON)]
        if i != 1:
            values = [
                v + jnp.where(spot == i // 2, added[i // 2, b : b + 1, :], 0.0)
                for b, v in enumerate(values)
            ]
        modes = real_dft(values)
        for k, mode in enumerate(modes):
            re, im = times(mode, twiddle[0, k, at, :], twiddle[1, k, at, :])
            lines[0, k, at, :] = re
            lines[1, k, at, :] = im
    zero = jnp.zeros((SUB, LEV), F32)
    for g in range(GROUPS):
        for part in range(2):
            stack = [lines[part, 4 * g + m] if 4 * g + m < MODES else zero for m in range(4)]
            for s, block in enumerate(swap_blocks(stack)):
                rhs[PAD * part + SUB * s : PAD * part + SUB * s + SUB, LEV * g : LEV * g + LEV] = block
    spectrum = three_products(forward, rhs[...])
    shape = (PAD, LEV * GROUPS)
    number = 4 * (lax.broadcasted_iota(jnp.int32, shape, 1) // LEV)
    number = number + (lax.broadcasted_iota(jnp.int32, shape, 1) // 32) % 4
    number = number + 32 * lax.broadcasted_iota(jnp.int32, shape, 0)
    kept = jnp.minimum(number, NLON - number).astype(F32) <= cut
    kept = jnp.concatenate([kept.astype(F32)] * 2, axis=0) > 0.5
    rhs[...] = three_products(backward, jnp.where(kept, spectrum, 0.0))
    for g in range(GROUPS):
        for part in range(2):
            stack = [
                rhs[PAD * part + SUB * s : PAD * part + SUB * s + SUB, LEV * g : LEV * g + LEV]
                for s in range(4)
            ]
            for m, block in enumerate(swap_blocks(stack)):
                if 4 * g + m < MODES:
                    lines[part, 4 * g + m] = block
    for i in range(SUB // 8):
        at = slice(8 * i, 8 * i + 8)
        modes = [
            times(
                (lines[0, k, at, :], lines[1, k, at, :]),
                back_twiddle[0, k, at, :],
                back_twiddle[1, k, at, :],
            )
            for k in range(MODES)
        ]
        for b, value in enumerate(real_inverse(modes)):
            out[b, at, :] = value


def outputs(
    lat, ret0, ret1, ret2, tr, wu, wv, ct, he, hw, n3, s3, early, ac,
    adv, gt, gu, gv, adjoint, low_stepped, top, bottom, adv_all, gt_all, gu_all, gv_all, sems,
):
    is0, is7 = lat[0] == 0, lat[0] == LAT - 1
    rets = (ret0, ret1, ret2)
    start = start_of(lat)

    def fill(i, carry):
        for m in range(10):
            adjoint[10 * i + m] = ct[10 * i + m]
        return carry

    lax.fori_loop(0, COLS // 10, fill, 0)
    adjoint[COLS] = he[1]
    adjoint[COLS + 1] = hw[1]

    @pl.when(is0 | is7)
    def _():
        flat = adjoint.reshape(PAD * ROWS, LEV)
        flat_stepped = low_stepped.reshape(PAD * ROWS, LEV)
        for k in range(POLAR):
            ret, kk = rets[k // 4], k % 4
            for target, base in ((flat, 0), (flat_stepped, 16)):
                line = swap_blocks([ret[base + 4 * kk + q] for q in range(4)])
                for s, part in enumerate(line):
                    target[pl.ds(SUB * s * ROWS + start + k, SUB, stride=ROWS), :] = part

    outer = jnp.where(is0, 0, ROWS - 1)
    mean = adjoint[COLS + 2, pl.ds(outer, 1), :]
    opposite = 2.0 * mean - line_of(adjoint, outer)
    early_north, early_south = lat[0] == 4, lat[0] == 3
    tr_north, north = (jnp.where(early_north, early[i], n3[i]) for i in range(2))
    tr_south, south = (jnp.where(early_south, early[i], s3[i]) for i in range(2))
    top[0] = jnp.where(is0, ac[0], tr_north)
    top[1] = jnp.where(is0, (0.125 - 0.5 * ac[1]) * opposite, north)
    bottom[0] = jnp.where(is7, ac[0], tr_south)
    bottom[1] = jnp.where(is7, (0.125 + 0.5 * ac[1]) * opposite, south)

    place = lax.broadcasted_iota(jnp.int32, (ROWS, LEV), 0)
    filtered = (is0 & (place < POLAR)) | (is7 & (place >= ROWS - POLAR))
    results = ((adv_all, adv), (gt_all, gt), (gu_all, gu), (gv_all, gv))

    def sent(step, i):
        block = pl.ds(step * CHUNK, CHUNK)
        return pltpu.make_async_copy(results[i][0].at[block], results[i][1].at[block], sems.at[step, i])

    for j in range(COLS):
        one = slice(j, j + 1)
        x, u, v, a = tr[j], wu[j], wv[j], adjoint[j]
        west, u_west, a_west = (
            (tr[j - 1], wu[j - 1], adjoint[j - 1]) if j else (hw[0], hw[2], adjoint[COLS + 1])
        )
        east, u_east = (tr[j + 1], wu[j + 1]) if j < COLS - 1 else (he[0], he[2])
        a_east = adjoint[j + 1]
        north, south = shifted(x, top[0, one, :], bottom[0, one, :])
        across, along = east - west, north - south
        stepped = (
            x - 0.5 * u * across - 0.5 * v * along + 0.125 * (east + west + north + south - 4.0 * x)
        )
        adv_all[j] = jnp.where(filtered, low_stepped[j], stepped)
        half = -0.5 * a
        gu_all[j] = across * half
        gv_all[j] = along * half
        place_north = jnp.where(
            place == 0, top[1, one, :], pltpu.roll((0.125 + 0.5 * v) * a, 1, 0)
        )
        place_south = jnp.where(
            place == ROWS - 1, bottom[1, one, :], pltpu.roll((0.125 - 0.5 * v) * a, ROWS - 1, 0)
        )
        gt_all[j] = (
            0.5 * a
            + (0.125 + 0.5 * u_east) * a_east
            + (0.125 - 0.5 * u_west) * a_west
            + place_north
            + place_south
        )
        if j % CHUNK == CHUNK - 1:
            for i in range(4):
                sent(j // CHUNK, i).start()
    for step in range(COLS // CHUNK):
        for i in range(4):
            sent(step, i).wait()


def whole(*shape):
    return pl.BlockSpec(shape, lambda i, *m: (0,) * len(shape))


OUTER_TILES = pl.BlockSpec(
    (COLS, 8, LEV), lambda i, lat, *m: (0, jnp.where(lat[0] == 0, 0, ROWS // 8 - 1), 0)
)
EDGE = whole(2, COLS, LEV)
ANYWHERE = pl.BlockSpec(memory_space=pl.ANY)


def call(kernel, name, scalars, in_specs, outs, cost, scratch=(), vmem=VMEM):
    return pl.pallas_call(
        kernel,
        name=name,
        grid_spec=pltpu.PrefetchScalarGridSpec(
            num_scalar_prefetch=scalars,
            grid=(1,),
            in_specs=in_specs,
            out_specs=[spec for _, spec in outs],
            scratch_shapes=list(scratch),
        ),
        out_shape=[jax.ShapeDtypeStruct(shape, F32) for shape, _ in outs],
        compiler_params=pltpu.CompilerParams(vmem_limit_bytes=vmem),
        cost_estimate=pl.CostEstimate(flops=cost, bytes_accessed=cost, transcendentals=0),
    )


def local_call(kernel, name, scalars, inputs, shapes, cost, scratch=(), out_space=pltpu.VMEM):
    return pl.pallas_call(
        kernel,
        name=name,
        in_specs=[pl.BlockSpec(memory_space=pltpu.SMEM)] * scalars
        + [pl.BlockSpec(memory_space=pltpu.VMEM)] * inputs,
        out_specs=[pl.BlockSpec(memory_space=out_space)] * len(shapes),
        scratch_shapes=list(scratch),
        out_shape=[jax.ShapeDtypeStruct(shape, F32) for shape in shapes],
        compiler_params=pltpu.CompilerParams(vmem_limit_bytes=VMEM),
        cost_estimate=pl.CostEstimate(flops=cost, bytes_accessed=cost, transcendentals=0),
    )


def moved(x, pairs):
    full = [(lon * LAT + a, lon * LAT + b) for lon in range(LON) for a, b in pairs]
    return lax.ppermute(x, ("lon", "lat"), full)


def body(tables, tracer, wind_u, wind_v, cotangent, cutoff):
    lat = lax.axis_index("lat").astype(jnp.int32).reshape(1)
    ring = [(i, (i + 1) % LON) for i in range(LON)]
    back_ring = [(b, a) for a, b in ring]
    opposite = [(i, (i + LON // 2) % LON) for i in range(LON)]
    tracer, wind_u, wind_v, cotangent = (
        jnp.transpose(f, (1, 0, 2)) for f in (tracer, wind_u, wind_v, cotangent)
    )
    chunk = (16, SUB, LEV)
    slabs = pltpu.VMEM((PAD, PITCH, LEV), F32)

    border = ((2, COLS, LEV), EDGE)
    (edge,) = call(
        pole_row, "pole_row", 1, [OUTER_TILES] * 2, [border], 1_000_000, vmem=60 * 1024 * 1024
    )(lat, tracer, wind_v)
    across = lax.ppermute(edge, "lon", opposite)
    *cot, ct_cols, ct_rows = local_call(
        pack_cotangent,
        "pack_cotangent",
        2,
        1,
        [chunk] * 3 + [(2, ROWS, LEV), (2, COLS, LEV)],
        1_000_000,
        [slabs],
    )(lat, cutoff, cotangent)
    cot_a, cot_b = moved(cot[1], SPREAD_A), moved(cot[2], SPREAD_B)

    *step, first_cols, last_cols, first_rows, last_rows, early_rows = local_call(
        pack_stepped,
        "pack_stepped",
        2,
        6,
        [chunk] * 3 + [(3, ROWS, LEV)] * 2 + [(2, COLS, LEV)] * 3,
        3_000_000,
        [slabs],
    )(lat, cutoff, tracer, wind_u, wind_v, across, ct_cols, ct_rows)
    step_a, step_b = moved(step[1], SPREAD_A), moved(step[2], SPREAD_B)
    east = lax.ppermute(first_cols, "lon", back_ring)
    west = lax.ppermute(last_cols, "lon", ring)
    early = moved(early_rows, EARLY)
    north, south = moved(last_rows, SOUTHWARD), moved(first_rows, NORTHWARD)
    (lines,) = call(
        pick, "pick", 1, [ANYWHERE] * 7, [((32, SUB, LEV), ANYWHERE)], 500_000,
        [pltpu.SemaphoreType.DMA((2,))],
    )(lat, cot[0], cot_a, cot_b, step[0], step_a, step_b, early)
    lines = lax.all_to_all(lines, "lon", 0, 0, tiled=True)

    low = pl.pallas_call(
        keep_low,
        name="keep_low",
        in_specs=[pl.BlockSpec(memory_space=pltpu.VMEM)] * 5,
        out_shape=jax.ShapeDtypeStruct((LON, SUB, LEV), F32),
        scratch_shapes=[
            pltpu.VMEM((2, MODES, SUB, LEV), F32),
            pltpu.VMEM((2 * PAD, LEV * GROUPS), F32),
            pltpu.VMEM((2, LON, LEV), F32),
        ],
        compiler_params=pltpu.CompilerParams(vmem_limit_bytes=VMEM),
        cost_estimate=pl.CostEstimate(flops=5_000_000, bytes_accessed=3_000_000, transcendentals=0),
    )(lines, *tables)
    back = lax.all_to_all(low, "lon", 0, 0, tiled=True)
    back_a = moved(back, [(b, a) for a, b in SPREAD_A])
    back_b = moved(back, [(b, a) for a, b in SPREAD_B])

    whole_block = (COLS, ROWS, LEV)
    results = local_call(
        outputs,
        "outputs",
        1,
        13,
        [whole_block] * 4,
        9_000_000,
        [pltpu.VMEM((PAD, ROWS, LEV), F32)] * 2
        + [pltpu.VMEM((2, COLS, LEV), F32)] * 2
        + [pltpu.VMEM(whole_block, F32)] * 4
        + [pltpu.SemaphoreType.DMA((COLS // CHUNK, 4))],
        out_space=pl.ANY,
    )(
        lat, back, back_a, back_b, tracer, wind_u, wind_v, cotangent, east, west, north, south,
        early, across,
    )
    return [jnp.transpose(r, (1, 0, 2)) for r in results]


def solution(mesh):
    field = P("lat", "lon", None)
    tables = tuple(jnp.asarray(t) for t in dft_tables())

    def run(*args):
        return jax.shard_map(
            lambda t, *a: tuple(body(t, *a)),
            mesh=mesh,
            in_specs=(P(), field, field, field, field, P("lat")),
            out_specs=(field,) * 4,
            check_vma=False,
        )(tables, *args)

    return run
```

```python
import functools

import jax
import jax.numpy as jnp
import ml_dtypes
import numpy as np
from jax import lax
from jax.experimental import pallas as pl
from jax.experimental.pallas import tpu as pltpu
from jax.sharding import PartitionSpec as P

F32 = jnp.float32
BF16 = jnp.bfloat16
LON, LAT = 32, 8
ROWS, COLS, LEV = 24, 90, 128
NLON = LON * COLS
POLAR = 12
MODES = LON // 2 + 1
PAD = 96
SUB = PAD // 4
GROUPS = 5
VMEM = 32 * 1024 * 1024
WINDOW = 16
PITCH = 24
CHUNK = 15

SPREAD_A = ((0, 3), (7, 4))
SPREAD_B = ((0, 1), (7, 6))
EARLY = ((3, 4), (4, 3))
SOUTHWARD = ((0, 1), (1, 2), (2, 3), (4, 5), (5, 6), (6, 7))
NORTHWARD = ((1, 0), (2, 1), (3, 2), (5, 4), (6, 5), (7, 6))


def dft_tables():
    place = np.arange(PAD)
    inside = place < COLS
    wave = np.arange(PAD)
    angle = 2 * np.pi * (wave[:, None] * place[None, :] % COLS) / COLS
    live = (wave[:, None] < COLS) & inside[None, :]
    cos, sin = np.where(live, np.cos(angle), 0), np.where(live, np.sin(angle), 0)
    forward = np.block([[cos, sin], [-sin, cos]])

    where = np.where(inside, place, 0)
    where[91] = -1
    where[90] = COLS
    valid = place < COLS + 2
    back_angle = 2 * np.pi * (where[:, None] * wave[None, :] % COLS) / COLS
    back_live = valid[:, None] & (wave[None, :] < COLS)
    bcos, bsin = np.where(back_live, np.cos(back_angle), 0), np.where(back_live, np.sin(back_angle), 0)
    bcos[92, 0] = 1.0
    backward = np.block([[bcos, -bsin], [bsin, bcos]]) / NLON

    def packed(values):
        spread = values.reshape(MODES, 4, SUB).transpose(0, 2, 1)
        return np.repeat(spread, 32, axis=2).astype(np.float32)

    mode = np.arange(MODES)
    turn = 2 * np.pi * (mode[:, None] * np.where(inside, place, 0)[None, :] % NLON) / NLON
    back_turn = 2 * np.pi * (mode[:, None] * where[None, :] % NLON) / NLON
    back_on = np.where(valid[None, :], 1.0, 0.0) * np.ones((MODES, 1))
    back_on[0, 92] = 1.0
    twiddle = np.stack([packed(np.cos(turn)), packed(-np.sin(turn))])
    back_twiddle = np.stack([packed(np.cos(back_turn) * back_on), packed(np.sin(back_turn) * back_on)])

    def split(matrix):
        high = matrix.astype(ml_dtypes.bfloat16)
        low = (matrix - high.astype(np.float64)).astype(ml_dtypes.bfloat16)
        return np.stack([high, low]).astype(np.float32)

    return split(forward), split(backward), twiddle, back_twiddle


def swap_blocks(parts):
    lane = lax.broadcasted_iota(jnp.int32, parts[0].shape, 1)
    low_half, even_block = lane < 64, (lane // 32) % 2 == 0
    first = [None] * 4
    for i in (0, 1):
        a, b = parts[i], parts[i + 2]
        first[i] = jnp.where(low_half, a, pltpu.roll(b, 64, 1))
        first[i + 2] = jnp.where(low_half, pltpu.roll(a, 64, 1), b)
    second = [None] * 4
    for i in (0, 2):
        a, b = first[i], first[i + 1]
        second[i] = jnp.where(even_block, a, pltpu.roll(b, 32, 1))
        second[i + 1] = jnp.where(even_block, pltpu.roll(a, 96, 1), b)
    return second


def start_of(lat):
    return jnp.where(lat[0] == 0, 0, ROWS - POLAR)


def window_of(lat):
    return pl.multiple_of(jnp.where(lat[0] == 0, 0, ROWS - WINDOW), 8)


def line_of(ref, row, count=COLS, first=0):
    rows = ref.shape[1]
    flat = ref.reshape(ref.shape[0] * rows, LEV)
    start, whole_tiles = first * rows + row, count // 8 * 8
    line = flat[pl.ds(start, whole_tiles, stride=rows), :]
    rest = [flat[pl.ds(start + j * rows, 1), :] for j in range(whole_tiles, count)]
    return jnp.concatenate([line] + rest, axis=0) if rest else line


def shifted(x, above, below):
    rows = x.shape[0]
    place = lax.broadcasted_iota(jnp.int32, x.shape, 0)
    north = jnp.where(place == 0, above, pltpu.roll(x, 1, 0))
    south = jnp.where(place == rows - 1, below, pltpu.roll(x, rows - 1, 0))
    return north, south


def pack_rows(lat, cutoff, slabs, outs):
    first = start_of(lat) - window_of(lat)
    place = lax.broadcasted_iota(jnp.int32, (WINDOW, LEV), 0)
    cuts = jnp.zeros((WINDOW, LEV), F32)
    for k in range(POLAR):
        cuts = jnp.where(place == first + k, cutoff[start_of(lat) + k].astype(F32), cuts)
    slabs[PAD - 2, 0:WINDOW, :] = jnp.zeros((WINDOW, LEV), F32)
    slabs[PAD - 1, 0:WINDOW, :] = cuts
    for k in range(POLAR):
        parts = [line_of(slabs, first + k, SUB, SUB * s) for s in range(4)]
        for q, part in enumerate(swap_blocks(parts)):
            outs[k // 4][4 * (k % 4) + q] = part


def pole_row(lat, tr, wv, edge):
    outer = jnp.where(lat[0] == 0, 0, 7)
    edge[0] = line_of(tr, outer)
    edge[1] = line_of(wv, outer)


def pack_cotangent(lat, cutoff, ct, out0, out1, out2, cols, border, slabs):
    rows = pl.ds(window_of(lat), WINDOW)
    for j in range(COLS):
        slabs[j, 0:WINDOW, :] = ct[j, rows, :]
    for j in range(COLS, PAD - 2):
        slabs[j, 0:WINDOW, :] = jnp.zeros((WINDOW, LEV), F32)
    pack_rows(lat, cutoff, slabs, (out0, out1, out2))
    cols[0] = ct[0]
    cols[1] = ct[COLS - 1]
    border[0] = line_of(ct, 0)
    border[1] = line_of(ct, ROWS - 1)


def pack_stepped(
    lat, cutoff, tr, wu, wv, ac, ct_cols, ct_rows,
    out0, out1, out2, first_cols, last_cols, first_rows, last_rows, early_rows, slabs,
):
    rows = pl.ds(window_of(lat), WINDOW)

    def step(j, east, west):
        x = tr[j, rows, :]
        beyond = ac[0, pl.ds(j, 1), :]
        north, south = shifted(x, beyond, beyond)
        slabs[j, 0:WINDOW, :] = (
            x
            - 0.5 * wu[j, rows, :] * (east - west)
            - 0.5 * wv[j, rows, :] * (north - south)
            + 0.125 * (east + west + north + south - 4.0 * x)
        )

    def middle(i, carry):
        for m in range(8):
            j = 8 * i + m + 1
            step(j, tr[j + 1, rows, :], tr[j - 1, rows, :])
        return carry

    nothing = jnp.zeros((WINDOW, LEV), F32)
    step(0, tr[1, rows, :], nothing)
    lax.fori_loop(0, (COLS - 2) // 8, middle, 0)
    step(COLS - 1, nothing, tr[COLS - 2, rows, :])
    slabs[COLS, 0:WINDOW, :] = tr[0, rows, :]
    slabs[COLS + 1, 0:WINDOW, :] = tr[COLS - 1, rows, :]
    slabs[COLS + 2, 0:WINDOW, :] = 0.125 + 0.5 * wu[0, rows, :]
    slabs[COLS + 3, 0:WINDOW, :] = 0.125 - 0.5 * wu[COLS - 1, rows, :]
    pack_rows(lat, cutoff, slabs, (out0, out1, out2))
    for i, (j, out) in enumerate(((0, first_cols), (COLS - 1, last_cols))):
        out[0] = tr[j]
        out[1] = ct_cols[i]
        out[2] = wu[j]
    first_rows[0] = line_of(tr, 0)
    last_rows[0] = line_of(tr, ROWS - 1)
    first_rows[1] = (0.125 - 0.5 * line_of(wv, 0)) * ct_rows[0]
    last_rows[1] = (0.125 + 0.5 * line_of(wv, ROWS - 1)) * ct_rows[1]
    for i in range(2):
        early_rows[i] = jnp.where(lat[0] == 3, last_rows[i], first_rows[i])


def times(a, cos, sin):
    if isinstance(sin, float) and sin == 0.0:
        return (a[0] * cos, None if a[1] is None else a[1] * cos) if cos != 1.0 else a
    if a[1] is None:
        return a[0] * cos, a[0] * sin
    return a[0] * cos - a[1] * sin, a[0] * sin + a[1] * cos


def plus(a, b):
    im = b[1] if a[1] is None else (a[1] if b[1] is None else a[1] + b[1])
    return a[0] + b[0], im


def minus(a, b):
    if a[1] is None:
        im = None if b[1] is None else -b[1]
    else:
        im = a[1] if b[1] is None else a[1] - b[1]
    return a[0] - b[0], im


def conj(a):
    return a[0], None if a[1] is None else -a[1]


def quarter(a, sign):
    re, im = a
    return (None if im is None else -sign * im), sign * re


def turned(a, k, n, sign):
    if k == 0:
        return a
    if 4 * k == n:
        re = jnp.zeros_like(a[0]) if a[1] is None else (-a[1] if sign > 0 else a[1])
        return re, (a[0] if sign > 0 else -a[0])
    return times(a, float(np.cos(2 * np.pi * k / n)), float(sign * np.sin(2 * np.pi * k / n)))


def real_dft(values):
    n = len(values)
    if n == 1:
        return [(values[0], None)]
    even, odd = real_dft(values[0::2]), real_dft(values[1::2])
    out = [None] * (n // 2 + 1)
    for k in range(n // 4 + 1):
        t = turned(odd[k], k, n, -1)
        out[k] = plus(even[k], t)
        if n // 2 - k != k:
            out[n // 2 - k] = conj(minus(even[k], t))
    return out


def real_inverse(modes):
    n = 2 * (len(modes) - 1)
    if n == 2:
        return [modes[0][0] + modes[1][0], modes[0][0] - modes[1][0]]
    even, odd = [], []
    for k in range(n // 4 + 1):
        a, b = modes[k], conj(modes[n // 2 - k])
        even.append(plus(a, b))
        odd.append(turned(minus(a, b), k, n, 1))
    out = [None] * n
    out[0::2], out[1::2] = real_inverse(even), real_inverse(odd)
    return out


def three_products(matrix, x):
    high = x.astype(BF16)
    low = (x - high.astype(F32)).astype(BF16)
    dot = functools.partial(jnp.dot, preferred_element_type=F32)
    main, rest = matrix[0].astype(BF16), matrix[1].astype(BF16)
    return dot(main, high) + (dot(main, low) + dot(rest, high))


def pick(lat, own_c, a_c, b_c, own_s, a_s, b_s, early, out, sems):
    polar = (lat[0] == 0) | (lat[0] == LAT - 1)
    in_a = (lat[0] == 3) | (lat[0] == LAT - 4)

    def copies(c, s):
        return [
            pltpu.make_async_copy(c, out.at[pl.ds(0, 16)], sems.at[0]),
            pltpu.make_async_copy(s, out.at[pl.ds(16, 16)], sems.at[1]),
        ]

    for chosen, c, s in (
        (polar, own_c, own_s),
        (in_a, a_c, a_s),
        (jnp.logical_not(polar | in_a), b_c, b_s),
    ):

        @pl.when(chosen)
        def _():
            for copy in copies(c, s):
                copy.start()

    for copy in copies(own_c, own_s):
        copy.wait()


def keep_low(x, forward, backward, twiddle, back_twiddle, out, lines, rhs, added):
    lane = lax.broadcasted_iota(jnp.int32, (8, LEV), 1)
    spot = lax.broadcasted_iota(jnp.int32, (8, LEV), 0)
    cut = jnp.max(jnp.where((lane >= 96) & (spot == 7), x[0, SUB - 8 : SUB, :], 0.0))
    wide = lax.broadcasted_iota(jnp.int32, (LON, LEV), 1)
    from_west = line_of(x, 20, LON) * pltpu.roll(line_of(x, 19, LON), 1, 0)
    added[0] = jnp.where(wide < 32, pltpu.roll(from_west, 32, 1), 0.0)
    from_east = line_of(x, 21, LON) * pltpu.roll(line_of(x, 18, LON), LON - 1, 0)
    added[1] = jnp.where(wide >= 96, from_east, 0.0)
    for i in range(SUB // 8):
        at = slice(8 * i, 8 * i + 8)
        values = [x[b, at, :] for b in range(LON)]
        if i != 1:
            values = [
                v + jnp.where(spot == i // 2, added[i // 2, b : b + 1, :], 0.0)
                for b, v in enumerate(values)
            ]
        modes = real_dft(values)
        for k, mode in enumerate(modes):
            re, im = times(mode, twiddle[0, k, at, :], twiddle[1, k, at, :])
            lines[0, k, at, :] = re
            lines[1, k, at, :] = im
    zero = jnp.zeros((SUB, LEV), F32)
    for g in range(GROUPS):
        for part in range(2):
            stack = [lines[part, 4 * g + m] if 4 * g + m < MODES else zero for m in range(4)]
            for s, block in enumerate(swap_blocks(stack)):
                rhs[PAD * part + SUB * s : PAD * part + SUB * s + SUB, LEV * g : LEV * g + LEV] = block
    spectrum = three_products(forward, rhs[...])
    shape = (PAD, LEV * GROUPS)
    number = 4 * (lax.broadcasted_iota(jnp.int32, shape, 1) // LEV)
    number = number + (lax.broadcasted_iota(jnp.int32, shape, 1) // 32) % 4
    number = number + 32 * lax.broadcasted_iota(jnp.int32, shape, 0)
    kept = jnp.minimum(number, NLON - number).astype(F32) <= cut
    kept = jnp.concatenate([kept.astype(F32)] * 2, axis=0) > 0.5
    rhs[...] = three_products(backward, jnp.where(kept, spectrum, 0.0))
    for g in range(GROUPS):
        for part in range(2):
            stack = [
                rhs[PAD * part + SUB * s : PAD * part + SUB * s + SUB, LEV * g : LEV * g + LEV]
                for s in range(4)
            ]
            for m, block in enumerate(swap_blocks(stack)):
                if 4 * g + m < MODES:
                    lines[part, 4 * g + m] = block
    for i in range(SUB // 8):
        at = slice(8 * i, 8 * i + 8)
        modes = [
            times(
                (lines[0, k, at, :], lines[1, k, at, :]),
                back_twiddle[0, k, at, :],
                back_twiddle[1, k, at, :],
            )
            for k in range(MODES)
        ]
        for b, value in enumerate(real_inverse(modes)):
            out[b, at, :] = value


def outputs(
    lat, ret0, ret1, ret2, tr, wu, wv, ct, he, hw, n3, s3, early, ac,
    adv, gt, gu, gv, adjoint, low_stepped, top, bottom, adv_all, gt_all, gu_all, gv_all, sems,
):
    is0, is7 = lat[0] == 0, lat[0] == LAT - 1
    rets = (ret0, ret1, ret2)
    start = start_of(lat)

    def fill(i, carry):
        for m in range(10):
            adjoint[10 * i + m] = ct[10 * i + m]
        return carry

    lax.fori_loop(0, COLS // 10, fill, 0)
    adjoint[COLS] = he[1]
    adjoint[COLS + 1] = hw[1]

    @pl.when(is0 | is7)
    def _():
        flat = adjoint.reshape(PAD * ROWS, LEV)
        flat_stepped = low_stepped.reshape(PAD * ROWS, LEV)
        for k in range(POLAR):
            ret, kk = rets[k // 4], k % 4
            for target, base in ((flat, 0), (flat_stepped, 16)):
                line = swap_blocks([ret[base + 4 * kk + q] for q in range(4)])
                for s, part in enumerate(line):
                    target[pl.ds(SUB * s * ROWS + start + k, SUB, stride=ROWS), :] = part

    outer = jnp.where(is0, 0, ROWS - 1)
    mean = adjoint[COLS + 2, pl.ds(outer, 1), :]
    opposite = 2.0 * mean - line_of(adjoint, outer)
    early_north, early_south = lat[0] == 4, lat[0] == 3
    tr_north, north = (jnp.where(early_north, early[i], n3[i]) for i in range(2))
    tr_south, south = (jnp.where(early_south, early[i], s3[i]) for i in range(2))
    top[0] = jnp.where(is0, ac[0], tr_north)
    top[1] = jnp.where(is0, (0.125 - 0.5 * ac[1]) * opposite, north)
    bottom[0] = jnp.where(is7, ac[0], tr_south)
    bottom[1] = jnp.where(is7, (0.125 + 0.5 * ac[1]) * opposite, south)

    place = lax.broadcasted_iota(jnp.int32, (ROWS, LEV), 0)
    filtered = (is0 & (place < POLAR)) | (is7 & (place >= ROWS - POLAR))
    results = ((adv_all, adv), (gt_all, gt), (gu_all, gu), (gv_all, gv))

    def sent(step, i):
        block = pl.ds(step * CHUNK, CHUNK)
        return pltpu.make_async_copy(results[i][0].at[block], results[i][1].at[block], sems.at[step, i])

    for j in range(COLS):
        one = slice(j, j + 1)
        x, u, v, a = tr[j], wu[j], wv[j], adjoint[j]
        west, u_west, a_west = (
            (tr[j - 1], wu[j - 1], adjoint[j - 1]) if j else (hw[0], hw[2], adjoint[COLS + 1])
        )
        east, u_east = (tr[j + 1], wu[j + 1]) if j < COLS - 1 else (he[0], he[2])
        a_east = adjoint[j + 1]
        north, south = shifted(x, top[0, one, :], bottom[0, one, :])
        across, along = east - west, north - south
        stepped = (
            x - 0.5 * u * across - 0.5 * v * along + 0.125 * (east + west + north + south - 4.0 * x)
        )
        adv_all[j] = jnp.where(filtered, low_stepped[j], stepped)
        half = -0.5 * a
        gu_all[j] = across * half
        gv_all[j] = along * half
        place_north = jnp.where(
            place == 0, top[1, one, :], pltpu.roll((0.125 + 0.5 * v) * a, 1, 0)
        )
        place_south = jnp.where(
            place == ROWS - 1, bottom[1, one, :], pltpu.roll((0.125 - 0.5 * v) * a, ROWS - 1, 0)
        )
        gt_all[j] = (
            0.5 * a
            + (0.125 + 0.5 * u_east) * a_east
            + (0.125 - 0.5 * u_west) * a_west
            + place_north
            + place_south
        )
        if j % CHUNK == CHUNK - 1:
            for i in range(4):
                sent(j // CHUNK, i).start()
    for step in range(COLS // CHUNK):
        for i in range(4):
            sent(step, i).wait()


def whole(*shape):
    return pl.BlockSpec(shape, lambda i, *m: (0,) * len(shape))


OUTER_TILES = pl.BlockSpec(
    (COLS, 8, LEV), lambda i, lat, *m: (0, jnp.where(lat[0] == 0, 0, ROWS // 8 - 1), 0)
)
EDGE = whole(2, COLS, LEV)
ANYWHERE = pl.BlockSpec(memory_space=pl.ANY)


def call(kernel, name, scalars, in_specs, outs, cost, scratch=(), vmem=VMEM):
    return pl.pallas_call(
        kernel,
        name=name,
        grid_spec=pltpu.PrefetchScalarGridSpec(
            num_scalar_prefetch=scalars,
            grid=(1,),
            in_specs=in_specs,
            out_specs=[spec for _, spec in outs],
            scratch_shapes=list(scratch),
        ),
        out_shape=[jax.ShapeDtypeStruct(shape, F32) for shape, _ in outs],
        compiler_params=pltpu.CompilerParams(vmem_limit_bytes=vmem),
        cost_estimate=pl.CostEstimate(flops=cost, bytes_accessed=cost, transcendentals=0),
    )


def local_call(kernel, name, scalars, inputs, shapes, cost, scratch=(), out_space=pltpu.VMEM):
    return pl.pallas_call(
        kernel,
        name=name,
        in_specs=[pl.BlockSpec(memory_space=pltpu.SMEM)] * scalars
        + [pl.BlockSpec(memory_space=pltpu.VMEM)] * inputs,
        out_specs=[pl.BlockSpec(memory_space=out_space)] * len(shapes),
        scratch_shapes=list(scratch),
        out_shape=[jax.ShapeDtypeStruct(shape, F32) for shape in shapes],
        compiler_params=pltpu.CompilerParams(vmem_limit_bytes=VMEM),
        cost_estimate=pl.CostEstimate(flops=cost, bytes_accessed=cost, transcendentals=0),
    )


def moved(x, pairs):
    full = [(lon * LAT + a, lon * LAT + b) for lon in range(LON) for a, b in pairs]
    return lax.ppermute(x, ("lon", "lat"), full)


def body(tables, tracer, wind_u, wind_v, cotangent, cutoff):
    lat = lax.axis_index("lat").astype(jnp.int32).reshape(1)
    ring = [(i, (i + 1) % LON) for i in range(LON)]
    back_ring = [(b, a) for a, b in ring]
    opposite = [(i, (i + LON // 2) % LON) for i in range(LON)]
    tracer, wind_u, wind_v, cotangent = (
        jnp.transpose(f, (1, 0, 2)) for f in (tracer, wind_u, wind_v, cotangent)
    )
    chunk = (16, SUB, LEV)
    slabs = pltpu.VMEM((PAD, PITCH, LEV), F32)

    border = ((2, COLS, LEV), EDGE)
    (edge,) = call(
        pole_row, "pole_row", 1, [OUTER_TILES] * 2, [border], 1_000_000, vmem=60 * 1024 * 1024
    )(lat, tracer, wind_v)
    across = lax.ppermute(edge, "lon", opposite)
    *cot, ct_cols, ct_rows = local_call(
        pack_cotangent,
        "pack_cotangent",
        2,
        1,
        [chunk] * 3 + [(2, ROWS, LEV), (2, COLS, LEV)],
        1_000_000,
        [slabs],
    )(lat, cutoff, cotangent)
    cot_a, cot_b = moved(cot[1], SPREAD_A), moved(cot[2], SPREAD_B)

    *step, first_cols, last_cols, first_rows, last_rows, early_rows = local_call(
        pack_stepped,
        "pack_stepped",
        2,
        6,
        [chunk] * 3 + [(3, ROWS, LEV)] * 2 + [(2, COLS, LEV)] * 3,
        3_000_000,
        [slabs],
    )(lat, cutoff, tracer, wind_u, wind_v, across, ct_cols, ct_rows)
    step_a, step_b = moved(step[1], SPREAD_A), moved(step[2], SPREAD_B)
    east = lax.ppermute(first_cols, "lon", back_ring)
    west = lax.ppermute(last_cols, "lon", ring)
    early = moved(early_rows, EARLY)
    north, south = moved(last_rows, SOUTHWARD), moved(first_rows, NORTHWARD)
    (lines,) = call(
        pick, "pick", 1, [ANYWHERE] * 7, [((32, SUB, LEV), ANYWHERE)], 500_000,
        [pltpu.SemaphoreType.DMA((2,))],
    )(lat, cot[0], cot_a, cot_b, step[0], step_a, step_b, early)
    lines = lax.all_to_all(lines, "lon", 0, 0, tiled=True)

    low = pl.pallas_call(
        keep_low,
        name="keep_low",
        in_specs=[pl.BlockSpec(memory_space=pltpu.VMEM)] * 5,
        out_shape=jax.ShapeDtypeStruct((LON, SUB, LEV), F32),
        scratch_shapes=[
            pltpu.VMEM((2, MODES, SUB, LEV), F32),
            pltpu.VMEM((2 * PAD, LEV * GROUPS), F32),
            pltpu.VMEM((2, LON, LEV), F32),
        ],
        compiler_params=pltpu.CompilerParams(vmem_limit_bytes=VMEM),
        cost_estimate=pl.CostEstimate(flops=5_000_000, bytes_accessed=3_000_000, transcendentals=0),
    )(lines, *tables)
    back = lax.all_to_all(low, "lon", 0, 0, tiled=True)
    back_a = moved(back, [(b, a) for a, b in SPREAD_A])
    back_b = moved(back, [(b, a) for a, b in SPREAD_B])

    whole_block = (COLS, ROWS, LEV)
    results = local_call(
        outputs,
        "outputs",
        1,
        13,
        [whole_block] * 4,
        9_000_000,
        [pltpu.VMEM((PAD, ROWS, LEV), F32)] * 2
        + [pltpu.VMEM((2, COLS, LEV), F32)] * 2
        + [pltpu.VMEM(whole_block, F32)] * 4
        + [pltpu.SemaphoreType.DMA((COLS // CHUNK, 4))],
        out_space=pl.ANY,
    )(
        lat, back, back_a, back_b, tracer, wind_u, wind_v, cotangent, east, west, north, south,
        early, across,
    )
    return [jnp.transpose(r, (1, 0, 2)) for r in results]


def solution(mesh):
    field = P("lat", "lon", None)
    tables = tuple(jnp.asarray(t) for t in dft_tables())

    def run(*args):
        return jax.shard_map(
            lambda t, *a: tuple(body(t, *a)),
            mesh=mesh,
            in_specs=(P(), field, field, field, field, P("lat")),
            out_specs=(field,) * 4,
            check_vma=False,
        )(tables, *args)

    return run
```
